256 devices in a mesh: space: 8 (over z_hi, y), dp: 32 (over x, z_lo, core).
Axes of the slice: x: 4, y: 4, z: 8 (z_hi: 2, z_lo: 4; z = z_hi * 4 + z_lo), core: 2. Of those that a mesh axis runs over, the one named last changes fastest.
Arguments:
- features: bfloat16 [32, 48, 64, 8, 128], P('dp', None, 'space'), may hold values from -21 to 21
- upstream: bfloat16 [32, 48, 64, 8, 128], P('dp', None, 'space'), may hold values from -21 to 21
- weight_one: bfloat16 [48, 48, 3, 3, 3], replicated, may hold values from -0.15625 to 0.15625
- weight_two: bfloat16 [48, 48, 3, 3, 3], replicated, may hold values from -0.15625 to 0.15625
- norm_gain: float32 [48], replicated, may hold values from 0.25 to 1.75
- norm_bias: float32 [48], replicated, may hold values from -3 to 3
Outputs:
- grad_input: bfloat16 [32, 48, 64, 8, 128], P('dp', None, 'space')
- grad_one: float32 [48, 48, 3, 3, 3], replicated
- grad_two: float32 [48, 48, 3, 3, 3], replicated
- grad_gain: float32 [48], replicated
- grad_bias: float32 [48], replicated
The draws below stay inside these ranges and needn't reach their ends.
All inputs are finite; a program needn't handle non-finite values.
Results may differ from the reference program's by a relative error of at most 0.0029.
Values may be sent and summed in bfloat16 or wider, within the bound.
A program may use at most 128 MiB of HBM per device.

```python
import jax
import jax.numpy as jnp
from jax import lax

C = 48
NX = 8
NY = 128
SAMPLES = 32
NZ = 64


def rough_field(key):
    key_base, key_rough, key_chan = jax.random.split(key, 3)
    shape = (SAMPLES, C, NZ, NX, NY)
    base = jax.random.truncated_normal(key_base, -3.0, 3.0, shape, jnp.float32)
    chan = jnp.exp(jax.random.uniform(key_chan, (1, C, 1, 1, 1), jnp.float32, -0.5, 0.5))
    rough = jnp.exp(jax.random.uniform(key_rough, shape, jnp.float32, -0.7, 0.7))
    ramp = (0.5 + jnp.arange(NZ, dtype=jnp.float32) / (NZ - 1)).reshape(1, 1, NZ, 1, 1)
    return (base * rough * chan * ramp).astype(jnp.bfloat16)


def draw_features(key, part):
    return rough_field(jax.random.fold_in(key, 11))


def draw_upstream(key, part):
    return rough_field(jax.random.fold_in(key, 23))


def normal_values(own_key, extent, spread, bound, kind=jnp.bfloat16):
    entries = spread * jax.random.normal(own_key, extent, jnp.float32)
    return jnp.clip(entries, min=-bound, max=bound).astype(kind)


def setup_inputs(seed: int = 0) -> dict:
    key_list = jax.random.split(jax.random.key(seed), 7)
    return {
        "features": draw_features(jax.random.fold_in(key_list[6], 71), 0),
        "upstream": draw_upstream(jax.random.fold_in(key_list[6], 71), 0),
        "weight_one": normal_values(key_list[2], (C, C, 3, 3, 3), (27 * C) ** -0.5, 0.15625),
        "weight_two": normal_values(key_list[3], (C, C, 3, 3, 3), (27 * C) ** -0.5, 0.15625),
        "norm_gain": jnp.clip(1.0 + 0.15 * jax.random.normal(key_list[4], (C,), jnp.float32), 0.25, 1.75),
        "norm_bias": normal_values(key_list[5], (C,), 0.5, 3.0, jnp.float32),
    }


epsilon = 1e-05

def conv_whole(field, kernel):
    return lax.conv_general_dilated(field, kernel, (1, 1, 1), ((1, 1), (1, 1), (1, 1)), dimension_numbers=('NCDHW', 'OIDHW', 'NCDHW'), precision=lax.Precision.HIGHEST)

def flipped(kernel):
    return jnp.transpose(kernel, (1, 0, 2, 3, 4))[:, :, ::-1, ::-1, ::-1]

def kernel_grad(source, target):
    padded = jnp.pad(source.astype(jnp.float32), ((0, 0), (0, 0), (1, 1), (1, 1), (1, 1)))
    target_f = target.astype(jnp.float32)
    depth_z = source.shape[2]
    depth_x = source.shape[3]
    depth_y = source.shape[4]
    pieces = []
    for shift_z in range(3):
        for shift_x in range(3):
            for shift_y in range(3):
                window = padded[:, :, shift_z:shift_z + depth_z, shift_x:shift_x + depth_x, shift_y:shift_y + depth_y]
                pieces.append(jnp.einsum('nizxy,nozxy->oi', window, target_f, precision=lax.Precision.HIGHEST))
    stacked = jnp.stack(pieces).reshape(3, 3, 3, source.shape[1], source.shape[1])
    return jnp.transpose(stacked, (3, 4, 0, 1, 2))

def reference(features, upstream, weight_one, weight_two, norm_gain, norm_bias):
    axes_cells = (2, 3, 4)
    pre_act = conv_whole(features.astype(jnp.float32), weight_one.astype(jnp.float32))
    mean_pre = lax.optimization_barrier(jnp.mean(pre_act, axis=axes_cells, keepdims=True))
    square_pre = lax.optimization_barrier(jnp.mean(pre_act * pre_act, axis=axes_cells, keepdims=True))
    inv_std = lax.rsqrt(square_pre - mean_pre * mean_pre + epsilon)
    normal_hat = (pre_act - mean_pre) * inv_std
    gain_b = norm_gain.reshape(1, -1, 1, 1, 1)
    normed = normal_hat * gain_b + norm_bias.reshape(1, -1, 1, 1, 1)
    sigmoid_val = jax.nn.sigmoid(normed)
    hidden = (normed * sigmoid_val).astype(jnp.bfloat16)
    grad_two = kernel_grad(hidden, upstream)
    grad_hidden = conv_whole(upstream.astype(jnp.float32), flipped(weight_two.astype(jnp.float32)))
    grad_norm = grad_hidden * sigmoid_val * (1.0 + normed * (1.0 - sigmoid_val))
    grad_bias = lax.optimization_barrier(jnp.sum(grad_norm, axis=(0, 2, 3, 4)))
    grad_gain = lax.optimization_barrier(jnp.sum(grad_norm * normal_hat, axis=(0, 2, 3, 4)))
    slope_one = lax.optimization_barrier(jnp.mean(grad_norm, axis=axes_cells, keepdims=True))
    slope_two = lax.optimization_barrier(jnp.mean(grad_norm * normal_hat, axis=axes_cells, keepdims=True))
    grad_pre = (gain_b * inv_std * (grad_norm - slope_one - normal_hat * slope_two)).astype(jnp.bfloat16)
    grad_one = kernel_grad(features, grad_pre)
    back = conv_whole(grad_pre.astype(jnp.float32), flipped(weight_one.astype(jnp.float32)))
    grad_input = (upstream.astype(jnp.float32) + back).astype(jnp.bfloat16)
    return (grad_input, grad_one, grad_two, grad_gain, grad_bias)
```

```python
import functools

import jax
import jax.numpy as jnp
from jax import lax
from jax.experimental import pallas as pl
from jax.experimental.pallas import tpu as pltpu
from jax.sharding import PartitionSpec as P

MESH = pl.DeviceIdType.MESH
F32 = jnp.float32
BF16 = jnp.bfloat16
C = 48
NZ, NX, NY = 8, 8, 128
CELLS = 64.0 * NX * NY
EPS = 1e-5
L = NX * NY
LP = L + 2 * NY
SZ_HI, SY, SX, SZ_LO = 2, 4, 4, 4
NXY = SX * SY
NZZ = SZ_HI * SZ_LO
NSP = SZ_HI * SY
ROWS = 512
HALF = ROWS // 2
PIECE = HALF // NXY


def dot(a, b):
    return lax.dot_general(a, b, (((1,), (0,)), ((), ())), preferred_element_type=F32)


def dot_nt(a, b):
    return lax.dot_general(a, b, (((1,), (1,)), ((), ())), preferred_element_type=F32)


def kernel(
    x_ref, g_ref, w1_ref, w2_ref, gain_ref, bias_ref,
    out_ref, g1_ref, g2_ref, gb_ref,
    xim, gim, him, pim, pre, gh, tmp, hx, hg, hp, w1c, w2f, w1f,
    st, acc, part, core_in, half_sum, xy_in, z_in, total,
    halo_send, halo_recv, st_send, st_recv, c_send, c_recv, xy_send, xy_recv, z_send, z_recv,
    ga_send, ga_recv, cg_send, cg_recv,
):
    sp = lax.axis_index("space")
    dp = lax.axis_index("dp")
    z_hi, y = sp // SY, sp % SY
    xx_, z_lo, core = dp // (SZ_LO * 2), (dp // 2) % SZ_LO, dp % 2
    me_xy = xx_ * SY + y
    me_z = z_hi * SZ_LO + z_lo
    sibling = (sp, dp + 1 - 2 * core)

    def sp_dev(j):
        return (j, dp)

    def xy_dev(j):
        return (z_hi * SY + j % SY, (j // SY) * (SZ_LO * 2) + z_lo * 2 + core)

    def z_dev(j):
        return ((j // SZ_LO) * SY + y, xx_ * (SZ_LO * 2) + (j % SZ_LO) * 2 + core)

    def others(count, me, body):
        def step(k, carry):
            body(lax.rem(me + k, count))
            return carry
        lax.fori_loop(1, count, step, 0)

    barrier = pltpu.get_barrier_semaphore()

    def greet(dev):
        pl.semaphore_signal(barrier, inc=1, device_id=dev, device_id_type=MESH)

    greet(sibling)
    others(NSP, sp, lambda j: greet(sp_dev(j)))
    others(NXY, me_xy, lambda j: greet(xy_dev(j)))
    others(NZZ, me_z, lambda j: greet(z_dev(j)))

    lane = lax.broadcasted_iota(jnp.int32, (C, NY), 1)
    eye = lax.broadcasted_iota(jnp.int32, (C, NY), 0) == lane
    first, last = lane == 0, lane == NY - 1

    def column(row):
        return jnp.sum(jnp.where(eye, jnp.broadcast_to(row, (C, NY)), 0.0), axis=1, keepdims=True)

    def as_row(col):
        return jnp.sum(jnp.where(eye, jnp.broadcast_to(col, (C, NY)), 0.0), axis=0, keepdims=True)

    def put(im, zi, lo, v):
        at = pl.ds(lo, NY)
        im[zi, 0:C, at] = jnp.where(first, 0.0, pltpu.roll(v, 1, 1)).astype(BF16)
        im[zi, C : 2 * C, at] = v.astype(BF16)
        im[zi, 2 * C : 3 * C, at] = jnp.where(last, 0.0, pltpu.roll(v, NY - 1, 1)).astype(BF16)

    def unpack(raw, im, zi, live):
        plane = raw.astype(F32)
        if live is not None:
            plane = jnp.where(live, plane, 0.0)
        tmp[...] = plane.reshape(C * NX, NY)
        for xb in range(NX):
            put(im, zi, NY * (xb + 1), tmp[pl.ds(xb, C, stride=NX), :])

    edge = jnp.zeros((3 * C, NY), BF16)

    def zero_edges(zi, carry):
        for im in (xim, gim, pim):
            im[zi, :, 0:NY] = edge
            im[zi, :, LP - NY : LP] = edge
        return carry

    lax.fori_loop(0, NZ + 2, zero_edges, 0)
    pim[0, C : 2 * C, :] = jnp.zeros((C, LP), BF16)
    pim[NZ + 1, C : 2 * C, :] = jnp.zeros((C, LP), BF16)

    def unpack_own(src, im):
        def step(zi, carry):
            unpack(src[:, pl.ds(zi, 1)].reshape(C, NX, NY), im, zi + 1, None)
            return carry
        lax.fori_loop(0, NZ, step, 0)

    unpack_own(x_ref, xim)

    for dz in range(3):
        rows = slice(dz * C, (dz + 1) * C)
        blocks = [w1_ref[dz * 9 + t].astype(F32).T for t in range(9)]
        w1c[rows, :] = jnp.concatenate(blocks, axis=0).T.astype(BF16)
        for w_ref, dst in ((w2_ref, w2f), (w1_ref, w1f)):
            blocks = [w_ref[26 - (dz * 9 + t)].astype(F32) for t in range(9)]
            dst[rows, :] = jnp.concatenate(blocks, axis=0).T.astype(BF16)

    pl.semaphore_wait(barrier, 1 + (NSP - 1) + (NXY - 1) + (NZZ - 1))

    has_up, has_down = sp < NSP - 1, sp > 0

    def halo_copy(src, dst, k, slot, dev):
        return pltpu.make_async_remote_copy(
            src_ref=src, dst_ref=dst.at[slot], send_sem=halo_send.at[k, slot],
            recv_sem=halo_recv.at[k, slot], device_id=dev, device_id_type=MESH,
        )

    def halo_start(low, high, dst, k):
        @pl.when(has_up)
        def _():
            halo_copy(high, dst, k, 0, (sp + 1, dp)).start()

        @pl.when(has_down)
        def _():
            halo_copy(low, dst, k, 1, (sp - 1, dp)).start()

    def halo_wait(low, high, dst, k):
        @pl.when(has_up)
        def _():
            halo_copy(high, dst, k, 0, (sp + 1, dp)).wait_send()
            halo_copy(high, dst, k, 1, (sp + 1, dp)).wait_recv()

        @pl.when(has_down)
        def _():
            halo_copy(low, dst, k, 1, (sp - 1, dp)).wait_send()
            halo_copy(low, dst, k, 0, (sp - 1, dp)).wait_recv()

    x_halo = (x_ref.at[:, 0], x_ref.at[:, NZ - 1], hx, 0)
    g_halo = (g_ref.at[:, 0], g_ref.at[:, NZ - 1], hg, 1)
    halo_start(*x_halo)
    halo_start(*g_halo)

    def window(im, zi):
        return jnp.concatenate([im[zi, :, NY * d : NY * d + L] for d in range(3)], axis=0)

    def conv_inner(im, w, dst):
        dst[0] = jnp.zeros((C, L), F32)
        dst[1] = jnp.zeros((C, L), F32)

        def step(zi, carry):
            p = dot(w[...], window(im, zi))
            dst[zi + 1] = p[0:C]
            dst[zi] += p[C : 2 * C]
            dst[zi - 1] += p[2 * C : 3 * C]
            return carry

        lax.fori_loop(1, NZ + 1, step, 0)

    def conv_faces(im, w, dst):
        dst[1] += dot(w[0:C], window(im, 0))
        dst[NZ] += dot(w[2 * C : 3 * C], window(im, NZ + 1))

    def face_planes(dst, im):
        unpack(dst[0], im, 0, has_down)
        unpack(dst[1], im, NZ + 1, has_up)

    def st_copy(k, j):
        return pltpu.make_async_remote_copy(
            src_ref=st.at[k, sp], dst_ref=st.at[k, sp], send_sem=st_send.at[k, j],
            recv_sem=st_recv.at[k, sp], device_id=sp_dev(j), device_id_type=MESH,
        )

    def st_wait(k, j):
        return pltpu.make_async_remote_copy(
            src_ref=st.at[k, j], dst_ref=st.at[k, j], send_sem=st_send.at[k, j],
            recv_sem=st_recv.at[k, j], device_id=sp_dev(j), device_id_type=MESH,
        )

    def st_start(k, one, two):
        row_one = as_row(jnp.sum(one, axis=1, keepdims=True))
        row_two = as_row(jnp.sum(two, axis=1, keepdims=True))
        lead = lax.broadcasted_iota(jnp.int32, (8, NY), 0)
        mine = jnp.where(lead == 0, row_one, 0.0) + jnp.where(lead == 1, row_two, 0.0)
        st[k, sp] = mine
        others(NSP, sp, lambda j: st_copy(k, j).start())
        return mine

    def st_finish(k):
        others(NSP, sp, lambda j: st_wait(k, j).wait_recv())
        others(NSP, sp, lambda j: st_copy(k, j).wait_send())
        s = st[k, 0]
        for j in range(1, NSP):
            s = s + st[k, j]
        return column(s[0:1] / CELLS), column(s[1:2] / CELLS)

    conv_inner(xim, w1c, pre)
    halo_wait(*x_halo)
    face_planes(hx, xim)
    conv_faces(xim, w1c, pre)

    zero = jnp.zeros((C, NY), F32)

    def moments(zi, carry):
        one, two = carry
        for xb in range(NX):
            v = pre[zi, :, NY * xb : NY * (xb + 1)]
            one, two = one + v, two + v * v
        return one, two

    st_start(0, *lax.fori_loop(1, NZ + 1, moments, (zero, zero)))

    unpack_own(g_ref, gim)
    conv_inner(gim, w2f, gh)
    halo_wait(*g_halo)
    face_planes(hg, gim)
    conv_faces(gim, w2f, gh)

    pad = jnp.zeros((1, NY - C), F32)
    gain = column(jnp.concatenate([gain_ref[...], pad], axis=1))
    bias = column(jnp.concatenate([bias_ref[...], pad], axis=1))
    mean, square = st_finish(0)
    inv_std = lax.rsqrt(square - mean * mean + EPS)

    def activate(zi, carry):
        one, two = carry
        for xb in range(NX):
            at = slice(NY * xb, NY * (xb + 1))
            hat = (pre[zi, :, at] - mean) * inv_std
            normed = hat * gain + bias
            sig = jax.nn.sigmoid(normed)
            put(him, zi - 1, NY * xb, (normed * sig).astype(BF16).astype(F32))
            gn = gh[zi, :, at] * sig * (1.0 + normed * (1.0 - sig))
            gh[zi, :, at] = gn
            pre[zi, :, at] = hat
            one, two = one + gn, two + gn * hat
        return one, two

    slopes = st_start(1, *lax.fori_loop(1, NZ + 1, activate, (zero, zero)))

    def c_copy(k):
        return pltpu.make_async_remote_copy(
            src_ref=part.at[k, pl.ds((1 - core) * HALF, HALF)], dst_ref=core_in.at[k],
            send_sem=c_send.at[k], recv_sem=c_recv.at[k], device_id=sibling, device_id_type=MESH,
        )

    def pack(k, tail):
        main = acc[:, 0:NY]
        part[k, 0 : 9 * C] = main
        rest = acc[:, NY : NY + 16]
        pieces = [rest[64 * r : 64 * (r + 1)] for r in range(6)]
        pieces.append(jnp.concatenate([rest[384:432], jnp.zeros((16, 16), F32)], axis=0))
        pieces.append(jnp.zeros((64, 16), F32))
        part[k, 9 * C : 9 * C + 64] = jnp.concatenate(pieces, axis=1)
        part[k, 496:504] = tail
        part[k, 504:512] = jnp.zeros((8, NY), F32)

    def core_start(k):
        c_copy(k).start()

    def xy_copy(k, j):
        return pltpu.make_async_remote_copy(
            src_ref=half_sum.at[k, pl.ds(j * PIECE, PIECE)], dst_ref=xy_in.at[k, me_xy],
            send_sem=xy_send.at[k, j], recv_sem=xy_recv.at[k, me_xy], device_id=xy_dev(j), device_id_type=MESH,
        )

    def xy_wait(k, j):
        return pltpu.make_async_remote_copy(
            src_ref=xy_in.at[k, j], dst_ref=xy_in.at[k, j],
            send_sem=xy_send.at[k, j], recv_sem=xy_recv.at[k, j], device_id=xy_dev(j), device_id_type=MESH,
        )

    def core_finish(k):
        c_copy(k).wait()
        half_sum[k] = part[k, pl.ds(core * HALF, HALF)] + core_in[k]
        others(NXY, me_xy, lambda j: xy_copy(k, j).start())

    def z_copy(k, j):
        return pltpu.make_async_remote_copy(
            src_ref=z_in.at[k, me_z], dst_ref=z_in.at[k, me_z],
            send_sem=z_send.at[k, j], recv_sem=z_recv.at[k, me_z], device_id=z_dev(j), device_id_type=MESH,
        )

    def z_wait(k, j):
        return pltpu.make_async_remote_copy(
            src_ref=z_in.at[k, j], dst_ref=z_in.at[k, j],
            send_sem=z_send.at[k, j], recv_sem=z_recv.at[k, j], device_id=z_dev(j), device_id_type=MESH,
        )

    def xy_finish(k):
        others(NXY, me_xy, lambda j: xy_wait(k, j).wait_recv())
        xy_in[k, me_xy] = half_sum[k, pl.ds(me_xy * PIECE, PIECE)]
        s = xy_in[k, 0]
        for j in range(1, NXY):
            s = s + xy_in[k, j]
        z_in[k, me_z] = s
        others(NZZ, me_z, lambda j: z_copy(k, j).start())

    def ga_at(j):
        return pl.ds(core * HALF + j * PIECE, PIECE)

    def ga_copy(k, j):
        return pltpu.make_async_remote_copy(
            src_ref=total.at[k, ga_at(me_xy)], dst_ref=total.at[k, ga_at(me_xy)],
            send_sem=ga_send.at[k, j], recv_sem=ga_recv.at[k, me_xy], device_id=xy_dev(j), device_id_type=MESH,
        )

    def ga_wait(k, j):
        return pltpu.make_async_remote_copy(
            src_ref=total.at[k, ga_at(j)], dst_ref=total.at[k, ga_at(j)],
            send_sem=ga_send.at[k, j], recv_sem=ga_recv.at[k, j], device_id=xy_dev(j), device_id_type=MESH,
        )

    def z_finish(k):
        others(NZZ, me_z, lambda j: z_wait(k, j).wait_recv())
        s = z_in[k, 0]
        for j in range(1, NZZ):
            s = s + z_in[k, j]
        total[k, ga_at(me_xy)] = s
        others(NXY, me_xy, lambda j: ga_copy(k, j).start())

    def cg_copy(k, which):
        at = pl.ds(which * HALF, HALF)
        return pltpu.make_async_remote_copy(
            src_ref=total.at[k, at], dst_ref=total.at[k, at],
            send_sem=cg_send.at[k], recv_sem=cg_recv.at[k], device_id=sibling, device_id_type=MESH,
        )

    def gather_finish(k):
        others(NXY, me_xy, lambda j: ga_wait(k, j).wait_recv())
        cg_copy(k, core).start()

    def drain(k):
        others(NXY, me_xy, lambda j: xy_copy(k, j).wait_send())
        others(NXY, me_xy, lambda j: ga_copy(k, j).wait_send())
        others(NZZ, me_z, lambda j: z_copy(k, j).wait_send())

    def all_finish(k, dst):
        cg_copy(k, core).wait_send()
        cg_copy(k, 1 - core).wait_recv()
        for b in range(9):
            m = total[k, b * C : (b + 1) * C]
            dst[3 * b] = m[:, 0:C]
            dst[3 * b + 1] = m[:, C : 2 * C]
            r, o = (b * C) // 64, (b * C) % 64
            rows = []
            left = C
            while left:
                n = min(64 - o, left)
                rows.append(total[k, 9 * C + o : 9 * C + o + n, 16 * r : 16 * (r + 1)])
                left -= n
                r, o = r + 1, 0
            tail = rows[0] if len(rows) == 1 else jnp.concatenate(rows, axis=0)
            dst[3 * b + 2] = jnp.concatenate([m[:, 2 * C : NY], tail], axis=1)

    acc[...] = jnp.zeros((9 * C, 3 * C), F32)

    def grad_two(zi, carry):
        lhs = jnp.concatenate(
            [
                gim[zi + 2 - dz, C : 2 * C, NY * (2 - dx) : NY * (2 - dx) + L]
                for dz in range(3)
                for dx in range(3)
            ],
            axis=0,
        )
        acc[...] += dot_nt(lhs, him[zi])
        return carry

    lax.fori_loop(0, NZ, grad_two, 0)
    pack(0, slopes)
    core_start(0)

    slope, slope_dot = st_finish(1)
    scale = gain * inv_std

    def before(zi, carry):
        for xb in range(NX):
            at = slice(NY * xb, NY * (xb + 1))
            gp = scale * (gh[zi, :, at] - slope - pre[zi, :, at] * slope_dot)
            put(pim, zi, NY * (xb + 1), gp.astype(BF16).astype(F32))
        return carry

    lax.fori_loop(1, NZ + 1, before, 0)
    p_halo = (pim.at[1, C : 2 * C, NY : NY + L], pim.at[NZ, C : 2 * C, NY : NY + L], hp, 2)
    halo_start(*p_halo)
    core_finish(0)

    acc[...] = jnp.zeros((9 * C, 3 * C), F32)

    def grad_one_rows(zi, dzs):
        return jnp.concatenate(
            [
                pim[zi + 1 - dz, C : 2 * C, NY * (2 - dx) : NY * (2 - dx) + L]
                for dz in dzs
                for dx in range(3)
            ],
            axis=0,
        )

    def grad_one(zi, carry):
        acc[...] += dot_nt(grad_one_rows(zi, range(3)), xim[zi, :, NY : NY + L])
        return carry

    lax.fori_loop(1, NZ + 1, grad_one, 0)
    acc[0 : 3 * C] += dot_nt(grad_one_rows(0, (0,)), xim[0, :, NY : NY + L])
    acc[6 * C : 9 * C] += dot_nt(grad_one_rows(NZ + 1, (2,)), xim[NZ + 1, :, NY : NY + L])
    pack(1, jnp.zeros((8, NY), F32))
    core_start(1)
    xy_finish(0)

    core_finish(1)
    conv_inner(pim, w1f, gh)
    z_finish(0)
    xy_finish(1)
    halo_wait(*p_halo)

    def face_plane(slot, zi, live):
        for xb in range(NX):
            v = hp[slot, :, NY * xb : NY * (xb + 1)].astype(F32)
            put(pim, zi, NY * (xb + 1), jnp.where(live, v, 0.0))

    face_plane(0, 0, has_down)
    face_plane(1, NZ + 1, has_up)
    conv_faces(pim, w1f, gh)
    z_finish(1)

    def finish(zi, carry):
        for xb in range(NX):
            v = gh[zi, :, NY * xb : NY * (xb + 1)]
            up = gim[zi, C : 2 * C, NY * (xb + 1) : NY * (xb + 2)]
            tmp[pl.ds(xb, C, stride=NX), :] = v + up.astype(F32)
        out_ref[:, pl.ds(zi - 1, 1)] = tmp[...].reshape(C, 1, NX, NY).astype(BF16)
        return carry

    lax.fori_loop(1, NZ + 1, finish, 0)
    gather_finish(0)
    gather_finish(1)
    all_finish(0, g2_ref)
    gb_ref[...] = total[0, 496:504]
    all_finish(1, g1_ref)
    drain(0)
    drain(1)


def local(features, upstream, weight_one, weight_two, norm_gain, norm_bias):
    w1 = jnp.transpose(weight_one, (2, 3, 4, 0, 1)).reshape(27, C, C)
    w2 = jnp.transpose(weight_two, (2, 3, 4, 0, 1)).reshape(27, C, C)
    vmem = pl.BlockSpec(memory_space=pltpu.VMEM)
    dma = pltpu.SemaphoreType.DMA
    out, g1, g2, gb = pl.pallas_call(
        kernel,
        out_shape=(
            jax.ShapeDtypeStruct((C, NZ, NX, NY), BF16),
            jax.ShapeDtypeStruct((27, C, C), F32),
            jax.ShapeDtypeStruct((27, C, C), F32),
            jax.ShapeDtypeStruct((8, NY), F32),
        ),
        in_specs=[vmem] * 6,
        out_specs=(vmem,) * 4,
        scratch_shapes=[
            pltpu.VMEM((NZ + 2, 3 * C, LP), BF16),
            pltpu.VMEM((NZ + 2, 3 * C, LP), BF16),
            pltpu.VMEM((NZ, 3 * C, L), BF16),
            pltpu.VMEM((NZ + 2, 3 * C, LP), BF16),
            pltpu.VMEM((NZ + 2, C, L), F32),
            pltpu.VMEM((NZ + 2, C, L), F32),
            pltpu.VMEM((C * NX, NY), F32),
            pltpu.VMEM((2, C, NX, NY), BF16),
            pltpu.VMEM((2, C, NX, NY), BF16),
            pltpu.VMEM((2, C, L), BF16),
            pltpu.VMEM((3 * C, 9 * C), BF16),
            pltpu.VMEM((3 * C, 9 * C), BF16),
            pltpu.VMEM((3 * C, 9 * C), BF16),
            pltpu.VMEM((2, NSP, 8, NY), F32),
            pltpu.VMEM((9 * C, 3 * C), F32),
            pltpu.VMEM((2, ROWS, NY), F32),
            pltpu.VMEM((2, HALF, NY), F32),
            pltpu.VMEM((2, HALF, NY), F32),
            pltpu.VMEM((2, NXY, PIECE, NY), F32),
            pltpu.VMEM((2, NZZ, PIECE, NY), F32),
            pltpu.VMEM((2, ROWS, NY), F32),
            dma((3, 2)), dma((3, 2)),
            dma((2, NSP)), dma((2, NSP)),
            dma((2,)), dma((2,)),
            dma((2, NXY)), dma((2, NXY)),
            dma((2, NZZ)), dma((2, NZZ)),
            dma((2, NXY)), dma((2, NXY)),
            dma((2,)), dma((2,)),
        ],
        compiler_params=pltpu.CompilerParams(
            collective_id=0, has_side_effects=True, vmem_limit_bytes=56 * 1024 * 1024
        ),
    )(
        features.reshape(C, NZ, NX, NY),
        upstream.reshape(C, NZ, NX, NY),
        w1,
        w2,
        norm_gain.reshape(1, C),
        norm_bias.reshape(1, C),
    )

    def grad(m):
        return jnp.transpose(m.reshape(3, 3, 3, C, C), (3, 4, 0, 1, 2))

    return out.reshape(1, C, NZ, NX, NY), grad(g1), grad(g2), gb[1, :C], gb[0, :C]


def solution(mesh):
    cells = P("dp", None, "space", None, None)
    return jax.shard_map(
        local,
        mesh=mesh,
        in_specs=(cells, cells, P(), P(), P(), P()),
        out_specs=(cells, P(), P(), P(), P()),
        check_vma=False,
    )
```

```python
import functools

import jax
import jax.numpy as jnp
from jax import lax
from jax.experimental import pallas as pl
from jax.experimental.pallas import tpu as pltpu
from jax.sharding import PartitionSpec as P

MESH = pl.DeviceIdType.MESH
F32 = jnp.float32
BF16 = jnp.bfloat16
C = 48
NZ, NX, NY = 8, 8, 128
CELLS = 64.0 * NX * NY
EPS = 1e-5
L = NX * NY
LP = L + 2 * NY
SZ_HI, SY, SX, SZ_LO = 2, 4, 4, 4
NXY = SX * SY
NZZ = SZ_HI * SZ_LO
NSP = SZ_HI * SY
ROWS = 512
HALF = ROWS // 2
PIECE = HALF // NXY


def dot(a, b):
    return lax.dot_general(a, b, (((1,), (0,)), ((), ())), preferred_element_type=F32)


def dot_nt(a, b):
    return lax.dot_general(a, b, (((1,), (1,)), ((), ())), preferred_element_type=F32)


def kernel(
    x_hbm, g_hbm, w1_hbm, w2_hbm, gain_ref, bias_ref,
    out_ref, total,
    x_ref, g_ref, w1_ref, w2_ref, load,
    xim, gim, him, pim, pre, gh, tmp, hx, hg, hp, w1c, w2f, w1f,
    st, acc, part, core_in, half_sum, xy_in, z_in,
    halo_send, halo_recv, st_send, st_recv, c_send, c_recv, xy_send, xy_recv, z_send, z_recv,
    ga_send, ga_recv, cg_send, cg_recv,
):
    sp = lax.axis_index("space")
    dp = lax.axis_index("dp")
    z_hi, y = sp // SY, sp % SY
    xx_, z_lo, core = dp // (SZ_LO * 2), (dp // 2) % SZ_LO, dp % 2
    me_xy = xx_ * SY + y
    me_z = z_hi * SZ_LO + z_lo
    sibling = (sp, dp + 1 - 2 * core)

    def sp_dev(j):
        return (j, dp)

    def xy_dev(j):
        return (z_hi * SY + j % SY, (j // SY) * (SZ_LO * 2) + z_lo * 2 + core)

    def z_dev(j):
        return ((j // SZ_LO) * SY + y, xx_ * (SZ_LO * 2) + (j % SZ_LO) * 2 + core)

    def others(count, me, body):
        def step(k, carry):
            body(lax.rem(me + k, count))
            return carry
        lax.fori_loop(1, count, step, 0)

    loads = [
        pltpu.make_async_copy(src, dst, load.at[i])
        for i, (src, dst) in enumerate(
            ((x_hbm, x_ref), (w1_hbm, w1_ref), (w2_hbm, w2_ref), (g_hbm, g_ref))
        )
    ]
    for each in loads:
        each.start()

    barrier = pltpu.get_barrier_semaphore()

    def greet(dev):
        pl.semaphore_signal(barrier, inc=1, device_id=dev, device_id_type=MESH)

    greet(sibling)
    others(NSP, sp, lambda j: greet(sp_dev(j)))
    others(NXY, me_xy, lambda j: greet(xy_dev(j)))
    others(NZZ, me_z, lambda j: greet(z_dev(j)))

    lane = lax.broadcasted_iota(jnp.int32, (C, NY), 1)
    eye = lax.broadcasted_iota(jnp.int32, (C, NY), 0) == lane
    first, last = lane == 0, lane == NY - 1

    def column(row):
        return jnp.sum(jnp.where(eye, jnp.broadcast_to(row, (C, NY)), 0.0), axis=1, keepdims=True)

    def as_row(col):
        return jnp.sum(jnp.where(eye, jnp.broadcast_to(col, (C, NY)), 0.0), axis=0, keepdims=True)

    def put_sides(im, zi, at, v):
        im[zi, 0:C, at] = jnp.where(first, 0.0, pltpu.roll(v, 1, 1)).astype(BF16)
        im[zi, 2 * C : 3 * C, at] = jnp.where(last, 0.0, pltpu.roll(v, NY - 1, 1)).astype(BF16)

    def put(im, zi, lo, v):
        at = pl.ds(lo, NY)
        im[zi, C : 2 * C, at] = v.astype(BF16)
        put_sides(im, zi, at, v)

    def sides(im, begin, lo):
        def step(zi, carry):
            for xb in range(NX):
                at = pl.ds(lo + NY * xb, NY)
                put_sides(im, zi, at, im[zi, C : 2 * C, at].astype(F32))
            return carry
        lax.fori_loop(begin, begin + NZ, step, 0)

    def unpack(raw, im, zi, live):
        plane = raw.astype(F32)
        if live is not None:
            plane = jnp.where(live, plane, 0.0)
        tmp[...] = plane.reshape(C * NX, NY)
        for xb in range(NX):
            put(im, zi, NY * (xb + 1), tmp[pl.ds(xb, C, stride=NX), :])

    edge = jnp.zeros((3 * C, NY), BF16)

    def zero_edges(zi, carry):
        for im in (xim, gim, pim):
            im[zi, :, 0:NY] = edge
            im[zi, :, LP - NY : LP] = edge
        return carry

    lax.fori_loop(0, NZ + 2, zero_edges, 0)
    pim[0, C : 2 * C, :] = jnp.zeros((C, LP), BF16)
    pim[NZ + 1, C : 2 * C, :] = jnp.zeros((C, LP), BF16)

    def unpack_own(src, im):
        def step(zi, carry):
            unpack(src[:, pl.ds(zi, 1)].reshape(C, NX, NY), im, zi + 1, None)
            return carry
        lax.fori_loop(0, NZ, step, 0)

    loads[0].wait()
    unpack_own(x_ref, xim)

    loads[1].wait()
    loads[2].wait()
    for dz in range(3):
        rows = slice(dz * C, (dz + 1) * C)
        blocks = [w1_ref[dz * 9 + t].astype(F32).T for t in range(9)]
        w1c[rows, :] = jnp.concatenate(blocks, axis=0).T.astype(BF16)
        for w_ref, dst in ((w2_ref, w2f), (w1_ref, w1f)):
            blocks = [w_ref[26 - (dz * 9 + t)].astype(F32) for t in range(9)]
            dst[rows, :] = jnp.concatenate(blocks, axis=0).T.astype(BF16)

    has_up, has_down = sp < NSP - 1, sp > 0

    def halo_copy(src, dst, k, slot, dev):
        return pltpu.make_async_remote_copy(
            src_ref=src, dst_ref=dst.at[slot], send_sem=halo_send.at[k, slot],
            recv_sem=halo_recv.at[k, slot], device_id=dev, device_id_type=MESH,
        )

    def halo_start(low, high, dst, k):
        @pl.when(has_up)
        def _():
            halo_copy(high, dst, k, 0, (sp + 1, dp)).start()

        @pl.when(has_down)
        def _():
            halo_copy(low, dst, k, 1, (sp - 1, dp)).start()

    def halo_wait(low, high, dst, k):
        @pl.when(has_up)
        def _():
            halo_copy(high, dst, k, 0, (sp + 1, dp)).wait_send()
            halo_copy(high, dst, k, 1, (sp + 1, dp)).wait_recv()

        @pl.when(has_down)
        def _():
            halo_copy(low, dst, k, 1, (sp - 1, dp)).wait_send()
            halo_copy(low, dst, k, 0, (sp - 1, dp)).wait_recv()

    x_halo = (x_ref.at[:, 0], x_ref.at[:, NZ - 1], hx, 0)
    g_halo = (g_ref.at[:, 0], g_ref.at[:, NZ - 1], hg, 1)

    def window(im, zi):
        return jnp.concatenate([im[zi, :, NY * d : NY * d + L] for d in range(3)], axis=0)

    def conv_inner(im, w, dst):
        dst[0] = jnp.zeros((C, L), F32)
        dst[1] = jnp.zeros((C, L), F32)

        def step(zi, carry):
            p = dot(w[...], window(im, zi))
            dst[zi + 1] = p[0:C]
            dst[zi] += p[C : 2 * C]
            dst[zi - 1] += p[2 * C : 3 * C]
            return carry

        lax.fori_loop(1, NZ + 1, step, 0)

    def conv_faces(im, w, dst):
        dst[1] += dot(w[0:C], window(im, 0))
        dst[NZ] += dot(w[2 * C : 3 * C], window(im, NZ + 1))

    def face_planes(dst, im):
        unpack(dst[0], im, 0, has_down)
        unpack(dst[1], im, NZ + 1, has_up)

    def st_copy(k, j):
        return pltpu.make_async_remote_copy(
            src_ref=st.at[k, sp], dst_ref=st.at[k, sp], send_sem=st_send.at[k, j],
            recv_sem=st_recv.at[k, sp], device_id=sp_dev(j), device_id_type=MESH,
        )

    def st_wait(k, j):
        return pltpu.make_async_remote_copy(
            src_ref=st.at[k, j], dst_ref=st.at[k, j], send_sem=st_send.at[k, j],
            recv_sem=st_recv.at[k, j], device_id=sp_dev(j), device_id_type=MESH,
        )

    def st_start(k, one, two):
        row_one = as_row(jnp.sum(one, axis=1, keepdims=True))
        row_two = as_row(jnp.sum(two, axis=1, keepdims=True))
        lead = lax.broadcasted_iota(jnp.int32, (8, NY), 0)
        mine = jnp.where(lead == 0, row_one, 0.0) + jnp.where(lead == 1, row_two, 0.0)
        st[k, sp] = mine
        others(NSP, sp, lambda j: st_copy(k, j).start())
        return mine

    def st_finish(k):
        others(NSP, sp, lambda j: st_wait(k, j).wait_recv())
        others(NSP, sp, lambda j: st_copy(k, j).wait_send())
        s = st[k, 0]
        for j in range(1, NSP):
            s = s + st[k, j]
        return column(s[0:1] / CELLS), column(s[1:2] / CELLS)

    conv_inner(xim, w1c, pre)
    loads[3].wait()
    unpack_own(g_ref, gim)
    pl.semaphore_wait(barrier, 1 + (NSP - 1) + (NXY - 1) + (NZZ - 1))

    halo_start(*x_halo)
    halo_start(*g_halo)
    conv_inner(gim, w2f, gh)
    halo_wait(*x_halo)
    face_planes(hx, xim)
    conv_faces(xim, w1c, pre)

    zero = jnp.zeros((C, NY), F32)

    def moments(zi, carry):
        one, two = carry
        for xb in range(NX):
            v = pre[zi, :, NY * xb : NY * (xb + 1)]
            one, two = one + v, two + v * v
        return one, two

    st_start(0, *lax.fori_loop(1, NZ + 1, moments, (zero, zero)))

    halo_wait(*g_halo)
    face_planes(hg, gim)
    conv_faces(gim, w2f, gh)

    pad = jnp.zeros((1, NY - C), F32)
    gain = column(jnp.concatenate([gain_ref[...], pad], axis=1))
    bias = column(jnp.concatenate([bias_ref[...], pad], axis=1))
    mean, square = st_finish(0)
    inv_std = lax.rsqrt(square - mean * mean + EPS)

    def activate(zi, carry):
        one, two = carry
        for xb in range(NX):
            at = slice(NY * xb, NY * (xb + 1))
            hat = (pre[zi, :, at] - mean) * inv_std
            normed = hat * gain + bias
            sig = jax.nn.sigmoid(normed)
            him[zi - 1, C : 2 * C, at] = (normed * sig).astype(BF16)
            gn = gh[zi, :, at] * sig * (1.0 + normed * (1.0 - sig))
            gh[zi, :, at] = gn
            pre[zi, :, at] = hat
            one, two = one + gn, two + gn * hat
        return one, two

    slopes = st_start(1, *lax.fori_loop(1, NZ + 1, activate, (zero, zero)))

    def c_copy(k):
        return pltpu.make_async_remote_copy(
            src_ref=part.at[k, pl.ds((1 - core) * HALF, HALF)], dst_ref=core_in.at[k],
            send_sem=c_send.at[k], recv_sem=c_recv.at[k], device_id=sibling, device_id_type=MESH,
        )

    def pack(k, tail):
        main = acc[:, 0:NY]
        part[k, 0 : 9 * C] = main
        rest = acc[:, NY : NY + 16]
        pieces = [rest[64 * r : 64 * (r + 1)] for r in range(6)]
        pieces.append(jnp.concatenate([rest[384:432], jnp.zeros((16, 16), F32)], axis=0))
        pieces.append(jnp.zeros((64, 16), F32))
        part[k, 9 * C : 9 * C + 64] = jnp.concatenate(pieces, axis=1)
        part[k, 496:504] = tail
        part[k, 504:512] = jnp.zeros((8, NY), F32)

    def core_start(k):
        c_copy(k).start()

    def xy_copy(k, j):
        return pltpu.make_async_remote_copy(
            src_ref=half_sum.at[k, pl.ds(j * PIECE, PIECE)], dst_ref=xy_in.at[k, me_xy],
            send_sem=xy_send.at[k, j], recv_sem=xy_recv.at[k, me_xy], device_id=xy_dev(j), device_id_type=MESH,
        )

    def xy_wait(k, j):
        return pltpu.make_async_remote_copy(
            src_ref=xy_in.at[k, j], dst_ref=xy_in.at[k, j],
            send_sem=xy_send.at[k, j], recv_sem=xy_recv.at[k, j], device_id=xy_dev(j), device_id_type=MESH,
        )

    def core_finish(k):
        c_copy(k).wait()
        half_sum[k] = part[k, pl.ds(core * HALF, HALF)] + core_in[k]
        others(NXY, me_xy, lambda j: xy_copy(k, j).start())

    def z_copy(k, j):
        return pltpu.make_async_remote_copy(
            src_ref=z_in.at[k, me_z], dst_ref=z_in.at[k, me_z],
            send_sem=z_send.at[k, j], recv_sem=z_recv.at[k, me_z], device_id=z_dev(j), device_id_type=MESH,
        )

    def z_wait(k, j):
        return pltpu.make_async_remote_copy(
            src_ref=z_in.at[k, j], dst_ref=z_in.at[k, j],
            send_sem=z_send.at[k, j], recv_sem=z_recv.at[k, j], device_id=z_dev(j), device_id_type=MESH,
        )

    def xy_finish(k):
        others(NXY, me_xy, lambda j: xy_wait(k, j).wait_recv())
        xy_in[k, me_xy] = half_sum[k, pl.ds(me_xy * PIECE, PIECE)]
        s = xy_in[k, 0]
        for j in range(1, NXY):
            s = s + xy_in[k, j]
        z_in[k, me_z] = s
        others(NZZ, me_z, lambda j: z_copy(k, j).start())

    def ga_at(j):
        return pl.ds(core * HALF + j * PIECE, PIECE)

    def ga_copy(k, j):
        return pltpu.make_async_remote_copy(
            src_ref=total.at[k, ga_at(me_xy)], dst_ref=total.at[k, ga_at(me_xy)],
            send_sem=ga_send.at[k, j], recv_sem=ga_recv.at[k, me_xy], device_id=xy_dev(j), device_id_type=MESH,
        )

    def ga_wait(k, j):
        return pltpu.make_async_remote_copy(
            src_ref=total.at[k, ga_at(j)], dst_ref=total.at[k, ga_at(j)],
            send_sem=ga_send.at[k, j], recv_sem=ga_recv.at[k, j], device_id=xy_dev(j), device_id_type=MESH,
        )

    def z_finish(k):
        others(NZZ, me_z, lambda j: z_wait(k, j).wait_recv())
        s = z_in[k, 0]
        for j in range(1, NZZ):
            s = s + z_in[k, j]
        total[k, ga_at(me_xy)] = s
        others(NXY, me_xy, lambda j: ga_copy(k, j).start())

    def cg_copy(k, which):
        at = pl.ds(which * HALF, HALF)
        return pltpu.make_async_remote_copy(
            src_ref=total.at[k, at], dst_ref=total.at[k, at],
            send_sem=cg_send.at[k], recv_sem=cg_recv.at[k], device_id=sibling, device_id_type=MESH,
        )

    def gather_finish(k):
        others(NXY, me_xy, lambda j: ga_wait(k, j).wait_recv())
        cg_copy(k, core).start()

    def drain(k):
        others(NXY, me_xy, lambda j: xy_copy(k, j).wait_send())
        others(NXY, me_xy, lambda j: ga_copy(k, j).wait_send())
        others(NZZ, me_z, lambda j: z_copy(k, j).wait_send())

    def all_finish(k):
        cg_copy(k, core).wait_send()
        cg_copy(k, 1 - core).wait_recv()

    sides(him, 0, 0)
    acc[...] = jnp.zeros((9 * C, 3 * C), F32)

    def shifted(im, zi, dzs):
        return jnp.concatenate(
            [
                im[zi + 1 - dz, C : 2 * C, NY * (2 - dx) : NY * (2 - dx) + L]
                for dz in dzs
                for dx in range(3)
            ],
            axis=0,
        )

    def pair(im, zi):
        return jnp.concatenate([shifted(im, zi, range(3)), shifted(im, zi + 1, range(3))], axis=1)

    def grad_two(i, carry):
        zi = 2 * i
        acc[...] += dot_nt(pair(gim, zi + 1), jnp.concatenate([him[zi], him[zi + 1]], axis=1))
        return carry

    lax.fori_loop(0, NZ // 2, grad_two, 0)
    pack(0, slopes)
    core_start(0)

    slope, slope_dot = st_finish(1)
    core_finish(0)
    scale = gain * inv_std

    def before(zi, carry):
        for xb in range(NX):
            at = slice(NY * xb, NY * (xb + 1))
            gp = scale * (gh[zi, :, at] - slope - pre[zi, :, at] * slope_dot)
            pim[zi, C : 2 * C, NY * (xb + 1) : NY * (xb + 2)] = gp.astype(BF16)
        return carry

    lax.fori_loop(1, NZ + 1, before, 0)
    p_halo = (pim.at[1, C : 2 * C, NY : NY + L], pim.at[NZ, C : 2 * C, NY : NY + L], hp, 2)
    halo_start(*p_halo)

    acc[...] = jnp.zeros((9 * C, 3 * C), F32)

    def grad_one(i, carry):
        zi = 2 * i + 1
        at = slice(NY, NY + L)
        acc[...] += dot_nt(pair(pim, zi), jnp.concatenate([xim[zi, :, at], xim[zi + 1, :, at]], axis=1))
        return carry

    lax.fori_loop(0, NZ // 2, grad_one, 0)
    acc[0 : 3 * C] += dot_nt(shifted(pim, 0, (0,)), xim[0, :, NY : NY + L])
    acc[6 * C : 9 * C] += dot_nt(shifted(pim, NZ + 1, (2,)), xim[NZ + 1, :, NY : NY + L])
    pack(1, jnp.zeros((8, NY), F32))
    core_start(1)

    sides(pim, 1, NY)
    core_finish(1)
    conv_inner(pim, w1f, gh)
    xy_finish(0)
    xy_finish(1)
    halo_wait(*p_halo)

    def face_plane(slot, zi, live):
        for xb in range(NX):
            v = hp[slot, :, NY * xb : NY * (xb + 1)].astype(F32)
            put(pim, zi, NY * (xb + 1), jnp.where(live, v, 0.0))

    face_plane(0, 0, has_down)
    face_plane(1, NZ + 1, has_up)
    conv_faces(pim, w1f, gh)

    def finish(zi, carry):
        for xb in range(NX):
            v = gh[zi, :, NY * xb : NY * (xb + 1)]
            up = gim[zi, C : 2 * C, NY * (xb + 1) : NY * (xb + 2)]
            tmp[pl.ds(xb, C, stride=NX), :] = v + up.astype(F32)
        out_ref[:, pl.ds(zi - 1, 1)] = tmp[...].reshape(C, 1, NX, NY).astype(BF16)
        return carry

    lax.fori_loop(1, NZ + 1, finish, 0)
    z_finish(0)
    z_finish(1)
    gather_finish(0)
    gather_finish(1)
    all_finish(0)
    all_finish(1)
    drain(0)
    drain(1)


def results(
    raw, total, out_ref, g1_ref, g2_ref, gain_ref, bias_ref, sem
):
    copy = pltpu.make_async_copy(raw, out_ref, sem)
    copy.start()
    for k, dst in ((0, g2_ref), (1, g1_ref)):
        for b in range(9):
            m = total[k, b * C : (b + 1) * C]
            dst[3 * b] = m[:, 0:C]
            dst[3 * b + 1] = m[:, C : 2 * C]
            r, o = (b * C) // 64, (b * C) % 64
            rows = []
            left = C
            while left:
                n = min(64 - o, left)
                rows.append(total[k, 9 * C + o : 9 * C + o + n, 16 * r : 16 * (r + 1)])
                left -= n
                r, o = r + 1, 0
            tail = rows[0] if len(rows) == 1 else jnp.concatenate(rows, axis=0)
            dst[3 * b + 2] = jnp.concatenate([m[:, 2 * C : NY], tail], axis=1)
    bias_ref[...] = total[0, 496:497, 0:C]
    gain_ref[...] = total[0, 497:498, 0:C]
    copy.wait()


def local(features, upstream, weight_one, weight_two, norm_gain, norm_bias):
    w1 = jnp.transpose(weight_one, (2, 3, 4, 0, 1)).reshape(27, C, C)
    w2 = jnp.transpose(weight_two, (2, 3, 4, 0, 1)).reshape(27, C, C)
    vmem = pl.BlockSpec(memory_space=pltpu.VMEM)
    dma = pltpu.SemaphoreType.DMA
    far = pl.BlockSpec(memory_space=pl.ANY)
    raw, total = pl.pallas_call(
        kernel,
        out_shape=(
            jax.ShapeDtypeStruct((C, NZ, NX, NY), BF16),
            jax.ShapeDtypeStruct((2, ROWS, NY), F32),
        ),
        in_specs=[far] * 4 + [vmem] * 2,
        out_specs=(vmem,) * 2,
        scratch_shapes=[
            pltpu.VMEM((C, NZ, NX, NY), BF16),
            pltpu.VMEM((C, NZ, NX, NY), BF16),
            pltpu.VMEM((27, C, C), BF16),
            pltpu.VMEM((27, C, C), BF16),
            dma((4,)),
            pltpu.VMEM((NZ + 2, 3 * C, LP), BF16),
            pltpu.VMEM((NZ + 2, 3 * C, LP), BF16),
            pltpu.VMEM((NZ, 3 * C, L), BF16),
            pltpu.VMEM((NZ + 2, 3 * C, LP), BF16),
            pltpu.VMEM((NZ + 2, C, L), F32),
            pltpu.VMEM((NZ + 2, C, L), F32),
            pltpu.VMEM((C * NX, NY), F32),
            pltpu.VMEM((2, C, NX, NY), BF16),
            pltpu.VMEM((2, C, NX, NY), BF16),
            pltpu.VMEM((2, C, L), BF16),
            pltpu.VMEM((3 * C, 9 * C), BF16),
            pltpu.VMEM((3 * C, 9 * C), BF16),
            pltpu.VMEM((3 * C, 9 * C), BF16),
            pltpu.VMEM((2, NSP, 8, NY), F32),
            pltpu.VMEM((9 * C, 3 * C), F32),
            pltpu.VMEM((2, ROWS, NY), F32),
            pltpu.VMEM((2, HALF, NY), F32),
            pltpu.VMEM((2, HALF, NY), F32),
            pltpu.VMEM((2, NXY, PIECE, NY), F32),
            pltpu.VMEM((2, NZZ, PIECE, NY), F32),
            dma((3, 2)), dma((3, 2)),
            dma((2, NSP)), dma((2, NSP)),
            dma((2,)), dma((2,)),
            dma((2, NXY)), dma((2, NXY)),
            dma((2, NZZ)), dma((2, NZZ)),
            dma((2, NXY)), dma((2, NXY)),
            dma((2,)), dma((2,)),
        ],
        compiler_params=pltpu.CompilerParams(
            collective_id=0, has_side_effects=True, vmem_limit_bytes=56 * 1024 * 1024
        ),
    )(
        features.reshape(C, NZ, NX, NY),
        upstream.reshape(C, NZ, NX, NY),
        w1,
        w2,
        norm_gain.reshape(1, C),
        norm_bias.reshape(1, C),
    )

    out, g1, g2, gain, bias = pl.pallas_call(
        results,
        out_shape=(
            jax.ShapeDtypeStruct((C, NZ, NX, NY), BF16),
            jax.ShapeDtypeStruct((27, C, C), F32),
            jax.ShapeDtypeStruct((27, C, C), F32),
            jax.ShapeDtypeStruct((1, C), F32),
            jax.ShapeDtypeStruct((1, C), F32),
        ),
        in_specs=[far, vmem],
        out_specs=(vmem,) * 5,
        scratch_shapes=[pltpu.SemaphoreType.DMA],
    )(raw, total)

    def grad(m):
        return jnp.transpose(m.reshape(3, 3, 3, C, C), (3, 4, 0, 1, 2))

    return out.reshape(1, C, NZ, NX, NY), grad(g1), grad(g2), gain.reshape(C), bias.reshape(C)


def solution(mesh):
    cells = P("dp", None, "space", None, None)
    return jax.shard_map(
        local,
        mesh=mesh,
        in_specs=(cells, cells, P(), P(), P(), P()),
        out_specs=(cells, P(), P(), P(), P()),
        check_vma=False,
    )
```

```python
import functools

import jax
import jax.numpy as jnp
from jax import lax
from jax.experimental import pallas as pl
from jax.experimental.pallas import tpu as pltpu
from jax.sharding import PartitionSpec as P

MESH = pl.DeviceIdType.MESH
F32 = jnp.float32
BF16 = jnp.bfloat16
C = 48
NZ, NX, NY = 8, 8, 128
CELLS = 64.0 * NX * NY
EPS = 1e-5
L = NX * NY
LP = L + 2 * NY
SZ_HI, SY, SX, SZ_LO = 2, 4, 4, 4
NXY = SX * SY
NZZ = SZ_HI * SZ_LO
NSP = SZ_HI * SY
ROWS = 512
HALF = ROWS // 2
PIECE = HALF // NXY


def dot(a, b):
    return lax.dot_general(a, b, (((1,), (0,)), ((), ())), preferred_element_type=F32)


def dot_nt(a, b):
    return lax.dot_general(a, b, (((1,), (1,)), ((), ())), preferred_element_type=F32)


def kernel(
    x_hbm, g_hbm, w1_hbm, w2_hbm, gain_hbm, bias_hbm,
    out_ref, total, g2_ref,
    x_ref, g_ref, w1_ref, w2_ref, gain_ref, bias_ref, load,
    xim, gim, him, pim, pre, gh, tmp, hx, hg, hp, w1c, w2f, w1f,
    st, acc, part, core_in, half_sum, xy_in, z_in,
    halo_send, halo_recv, st_send, st_recv, c_send, c_recv, xy_send, xy_recv, z_send, z_recv,
    ga_send, ga_recv, cg_send, cg_recv,
):
    sp = lax.axis_index("space")
    dp = lax.axis_index("dp")
    z_hi, y = sp // SY, sp % SY
    xx_, z_lo, core = dp // (SZ_LO * 2), (dp // 2) % SZ_LO, dp % 2
    me_xy = xx_ * SY + y
    me_z = z_hi * SZ_LO + z_lo
    sibling = (sp, dp + 1 - 2 * core)

    def sp_dev(j):
        return (j, dp)

    def xy_dev(j):
        return (z_hi * SY + j % SY, (j // SY) * (SZ_LO * 2) + z_lo * 2 + core)

    def z_dev(j):
        return ((j // SZ_LO) * SY + y, xx_ * (SZ_LO * 2) + (j % SZ_LO) * 2 + core)

    def others(count, me, body):
        def step(k, carry):
            body(lax.rem(me + k, count))
            return carry
        lax.fori_loop(1, count, step, 0)

    ys = [(y + o) % SY for o in range(SY)]
    xs = [(xx_ + o) % SX for o in range(SX)]
    hops = (0, 1, 2, 1)
    offsets = sorted(((a, b) for a in range(SX) for b in range(SY)), key=lambda o: -hops[o[0]] - hops[o[1]])
    xy_peers = [
        (xs[a] * SY + ys[b], (z_hi * SY + ys[b], xs[a] * (SZ_LO * 2) + z_lo * 2 + core))
        for a, b in offsets[:-1]
    ]
    sp_peers = [
        (side * SY + ys[b], (side * SY + ys[b], dp))
        for side, bs in ((1 - z_hi, (2, 1, 3, 0)), (z_hi, (2, 1, 3)))
        for b in bs
    ]
    z_ids = [(me_z + o) % NZZ for o in (4, 3, 5, 2, 6, 1, 7)]
    z_peers = [(j, z_dev(j)) for j in z_ids]

    loads = [
        pltpu.make_async_copy(src, dst, load.at[i])
        for i, (src, dst) in enumerate(
            ((x_hbm, x_ref), (w1_hbm, w1_ref), (w2_hbm, w2_ref), (g_hbm, g_ref), (gain_hbm, gain_ref), (bias_hbm, bias_ref))
        )
    ]
    for each in loads:
        each.start()

    barrier = pltpu.get_barrier_semaphore()

    def greet(dev):
        pl.semaphore_signal(barrier, inc=1, device_id=dev, device_id_type=MESH)

    for _, dev in sp_peers + z_peers + xy_peers:
        greet(dev)
    greet(sibling)

    lane = lax.broadcasted_iota(jnp.int32, (C, NY), 1)
    eye = lax.broadcasted_iota(jnp.int32, (C, NY), 0) == lane
    first, last = lane == 0, lane == NY - 1

    def column(row):
        return jnp.sum(jnp.where(eye, jnp.broadcast_to(row, (C, NY)), 0.0), axis=1, keepdims=True)

    def as_row(col):
        return jnp.sum(jnp.where(eye, jnp.broadcast_to(col, (C, NY)), 0.0), axis=0, keepdims=True)

    def put_sides(im, zi, at, v):
        im[zi, 0:C, at] = jnp.where(first, 0.0, pltpu.roll(v, 1, 1)).astype(BF16)
        im[zi, 2 * C : 3 * C, at] = jnp.where(last, 0.0, pltpu.roll(v, NY - 1, 1)).astype(BF16)

    def put(im, zi, lo, v):
        at = pl.ds(lo, NY)
        im[zi, C : 2 * C, at] = v.astype(BF16)
        put_sides(im, zi, at, v)

    def sides(im, begin, lo):
        def step(zi, carry):
            for xb in range(NX):
                at = pl.ds(lo + NY * xb, NY)
                put_sides(im, zi, at, im[zi, C : 2 * C, at].astype(F32))
            return carry
        lax.fori_loop(begin, begin + NZ, step, 0)

    def unpack(raw, im, zi):
        tmp[...] = raw.astype(F32).reshape(C * NX, NY)
        for xb in range(NX):
            put(im, zi, NY * (xb + 1), tmp[pl.ds(xb, C, stride=NX), :])

    edge = jnp.zeros((3 * C, NY), BF16)

    def zero_edges(zi, carry):
        for im in (xim, gim, pim):
            im[zi, :, 0:NY] = edge
            im[zi, :, LP - NY : LP] = edge
        return carry

    lax.fori_loop(0, NZ + 2, zero_edges, 0)
    pim[0, C : 2 * C, :] = jnp.zeros((C, LP), BF16)
    pim[NZ + 1, C : 2 * C, :] = jnp.zeros((C, LP), BF16)

    def unpack_own(src, im):
        def step(zi, carry):
            unpack(src[:, pl.ds(zi, 1)].reshape(C, NX, NY), im, zi + 1)
            return carry
        lax.fori_loop(0, NZ, step, 0)

    loads[0].wait()
    unpack_own(x_ref, xim)

    loads[1].wait()
    loads[2].wait()
    for dz in range(3):
        rows = slice(dz * C, (dz + 1) * C)
        blocks = [w1_ref[dz * 9 + t].astype(F32).T for t in range(9)]
        w1c[rows, :] = jnp.concatenate(blocks, axis=0).T.astype(BF16)
        for w_ref, dst in ((w2_ref, w2f), (w1_ref, w1f)):
            blocks = [w_ref[26 - (dz * 9 + t)].astype(F32) for t in range(9)]
            dst[rows, :] = jnp.concatenate(blocks, axis=0).T.astype(BF16)

    has_up, has_down = sp < NSP - 1, sp > 0

    def halo_copy(src, dst, k, slot, dev):
        return pltpu.make_async_remote_copy(
            src_ref=src, dst_ref=dst.at[slot], send_sem=halo_send.at[k, slot],
            recv_sem=halo_recv.at[k, slot], device_id=dev, device_id_type=MESH,
        )

    def halo_start(low, high, dst, k):
        @pl.when(has_up)
        def _():
            halo_copy(high, dst, k, 0, (sp + 1, dp)).start()

        @pl.when(has_down)
        def _():
            halo_copy(low, dst, k, 1, (sp - 1, dp)).start()

    def halo_wait(low, high, dst, k):
        @pl.when(has_up)
        def _():
            halo_copy(high, dst, k, 0, (sp + 1, dp)).wait_send()
            halo_copy(high, dst, k, 1, (sp + 1, dp)).wait_recv()

        @pl.when(has_down)
        def _():
            halo_copy(low, dst, k, 1, (sp - 1, dp)).wait_send()
            halo_copy(low, dst, k, 0, (sp - 1, dp)).wait_recv()

    def halo_of(im, dst, k):
        at = (slice(C, 2 * C), slice(NY, NY + L))
        return im.at[(1,) + at], im.at[(NZ,) + at], dst, k

    x_halo = halo_of(xim, hx, 0)
    g_halo = halo_of(gim, hg, 1)
    p_halo = halo_of(pim, hp, 2)

    def window(im, zi):
        return jnp.concatenate([im[zi, :, NY * d : NY * d + L] for d in range(3)], axis=0)

    def conv_inner(im, w, dst):
        dst[0] = jnp.zeros((C, L), F32)
        dst[1] = jnp.zeros((C, L), F32)

        def step(zi, carry):
            p = dot(w[...], window(im, zi))
            dst[zi + 1] = p[0:C]
            dst[zi] += p[C : 2 * C]
            dst[zi - 1] += p[2 * C : 3 * C]
            return carry

        lax.fori_loop(1, NZ + 1, step, 0)

    def conv_faces(im, w, dst):
        dst[1] += dot(w[0:C], window(im, 0))
        dst[NZ] += dot(w[2 * C : 3 * C], window(im, NZ + 1))

    def face_planes(dst, im):
        for slot, zi, live in ((0, 0, has_down), (1, NZ + 1, has_up)):
            for xb in range(NX):
                v = dst[slot, :, NY * xb : NY * (xb + 1)].astype(F32)
                put(im, zi, NY * (xb + 1), jnp.where(live, v, 0.0))

    def st_copy(k, j, dev):
        return pltpu.make_async_remote_copy(
            src_ref=st.at[k, sp], dst_ref=st.at[k, sp], send_sem=st_send.at[k, j],
            recv_sem=st_recv.at[k, sp], device_id=dev, device_id_type=MESH,
        )

    def st_wait(k, j):
        return pltpu.make_async_remote_copy(
            src_ref=st.at[k, j], dst_ref=st.at[k, j], send_sem=st_send.at[k, j],
            recv_sem=st_recv.at[k, j], device_id=sp_dev(j), device_id_type=MESH,
        )

    def st_start(k, one, two):
        row_one = as_row(jnp.sum(one, axis=1, keepdims=True))
        row_two = as_row(jnp.sum(two, axis=1, keepdims=True))
        lead = lax.broadcasted_iota(jnp.int32, (8, NY), 0)
        mine = jnp.where(lead == 0, row_one, 0.0) + jnp.where(lead == 1, row_two, 0.0)
        st[k, sp] = mine
        for j, dev in sp_peers:
            st_copy(k, j, dev).start()
        return mine

    def st_finish(k):
        others(NSP, sp, lambda j: st_wait(k, j).wait_recv())
        s = st[k, 0]
        for j in range(1, NSP):
            s = s + st[k, j]
        return column(s[0:1] / CELLS), column(s[1:2] / CELLS)

    conv_inner(xim, w1c, pre)
    loads[3].wait()
    unpack_own(g_ref, gim)
    pl.semaphore_wait(barrier, 1 + (NSP - 1) + (NXY - 1) + (NZZ - 1))

    halo_start(*x_halo)
    halo_start(*g_halo)
    conv_inner(gim, w2f, gh)

    zero = jnp.zeros((C, NY), F32)

    def moments(zi, carry):
        one, two = carry
        for xb in range(NX):
            v = pre[zi, :, NY * xb : NY * (xb + 1)]
            one, two = one + v, two + v * v
        return one, two

    sums = lax.fori_loop(2, NZ, moments, (zero, zero))
    halo_wait(*x_halo)
    face_planes(hx, xim)
    conv_faces(xim, w1c, pre)
    st_start(0, *moments(NZ, moments(1, sums)))

    halo_wait(*g_halo)
    face_planes(hg, gim)
    conv_faces(gim, w2f, gh)

    loads[4].wait()
    loads[5].wait()
    pad = jnp.zeros((1, NY - C), F32)
    gain = column(jnp.concatenate([gain_ref[...], pad], axis=1))
    bias = column(jnp.concatenate([bias_ref[...], pad], axis=1))
    mean, square = st_finish(0)
    inv_std = lax.rsqrt(square - mean * mean + EPS)

    def activate(zi, carry):
        one, two = carry
        for xb in range(NX):
            at = slice(NY * xb, NY * (xb + 1))
            hat = (pre[zi, :, at] - mean) * inv_std
            normed = hat * gain + bias
            sig = jax.nn.sigmoid(normed)
            him[zi - 1, C : 2 * C, at] = (normed * sig).astype(BF16)
            gn = gh[zi, :, at] * sig * (1.0 + normed * (1.0 - sig))
            gh[zi, :, at] = gn
            pre[zi, :, at] = hat
            one, two = one + gn, two + gn * hat
        return one, two

    slopes = st_start(1, *lax.fori_loop(1, NZ + 1, activate, (zero, zero)))

    def c_copy(k):
        return pltpu.make_async_remote_copy(
            src_ref=part.at[k, pl.ds((1 - core) * HALF, HALF)], dst_ref=core_in.at[k],
            send_sem=c_send.at[k], recv_sem=c_recv.at[k], device_id=sibling, device_id_type=MESH,
        )

    def pack(k, tail):
        main = acc[:, 0:NY]
        part[k, 0 : 9 * C] = main
        rest = acc[:, NY : NY + 16]
        pieces = [rest[64 * r : 64 * (r + 1)] for r in range(6)]
        pieces.append(jnp.concatenate([rest[384:432], jnp.zeros((16, 16), F32)], axis=0))
        pieces.append(jnp.zeros((64, 16), F32))
        part[k, 9 * C : 9 * C + 64] = jnp.concatenate(pieces, axis=1)
        part[k, 496:504] = tail
        part[k, 504:512] = jnp.zeros((8, NY), F32)

    def core_start(k):
        c_copy(k).start()

    def xy_copy(k, j, dev):
        return pltpu.make_async_remote_copy(
            src_ref=half_sum.at[k, pl.ds(j * PIECE, PIECE)], dst_ref=xy_in.at[k, me_xy],
            send_sem=xy_send.at[k, j], recv_sem=xy_recv.at[k, me_xy], device_id=dev, device_id_type=MESH,
        )

    def xy_wait(k, j):
        return pltpu.make_async_remote_copy(
            src_ref=xy_in.at[k, j], dst_ref=xy_in.at[k, j],
            send_sem=xy_send.at[k, j], recv_sem=xy_recv.at[k, j], device_id=xy_dev(j), device_id_type=MESH,
        )

    def core_finish(k):
        c_copy(k).wait_recv()
        half_sum[k] = part[k, pl.ds(core * HALF, HALF)] + core_in[k]
        for j, dev in xy_peers:
            xy_copy(k, j, dev).start()

    def z_copy(k, j, dev):
        return pltpu.make_async_remote_copy(
            src_ref=z_in.at[k, me_z], dst_ref=z_in.at[k, me_z],
            send_sem=z_send.at[k, j], recv_sem=z_recv.at[k, me_z], device_id=dev, device_id_type=MESH,
        )

    def z_wait(k, j):
        return pltpu.make_async_remote_copy(
            src_ref=z_in.at[k, j], dst_ref=z_in.at[k, j],
            send_sem=z_send.at[k, j], recv_sem=z_recv.at[k, j], device_id=z_dev(j), device_id_type=MESH,
        )

    def xy_finish(k):
        others(NXY, me_xy, lambda j: xy_wait(k, j).wait_recv())
        xy_in[k, me_xy] = half_sum[k, pl.ds(me_xy * PIECE, PIECE)]
        s = xy_in[k, 0]
        for j in range(1, NXY):
            s = s + xy_in[k, j]
        z_in[k, me_z] = s
        for j, dev in z_peers:
            z_copy(k, j, dev).start()

    def ga_at(j):
        return pl.ds(core * HALF + j * PIECE, PIECE)

    def ga_copy(k, j, dev):
        return pltpu.make_async_remote_copy(
            src_ref=total.at[k, ga_at(me_xy)], dst_ref=total.at[k, ga_at(me_xy)],
            send_sem=ga_send.at[k, j], recv_sem=ga_recv.at[k, me_xy], device_id=dev, device_id_type=MESH,
        )

    def ga_wait(k, j):
        return pltpu.make_async_remote_copy(
            src_ref=total.at[k, ga_at(j)], dst_ref=total.at[k, ga_at(j)],
            send_sem=ga_send.at[k, j], recv_sem=ga_recv.at[k, j], device_id=xy_dev(j), device_id_type=MESH,
        )

    def z_finish(k):
        others(NZZ, me_z, lambda j: z_wait(k, j).wait_recv())
        s = z_in[k, 0]
        for j in range(1, NZZ):
            s = s + z_in[k, j]
        total[k, ga_at(me_xy)] = s
        for j, dev in xy_peers:
            ga_copy(k, j, dev).start()

    def cg_copy(k, which):
        at = pl.ds(which * HALF, HALF)
        return pltpu.make_async_remote_copy(
            src_ref=total.at[k, at], dst_ref=total.at[k, at],
            send_sem=cg_send.at[k], recv_sem=cg_recv.at[k], device_id=sibling, device_id_type=MESH,
        )

    def gather_finish(k):
        others(NXY, me_xy, lambda j: ga_wait(k, j).wait_recv())
        cg_copy(k, core).start()

    def drain(k):
        others(NSP, sp, lambda j: st_copy(k, j, sp_dev(j)).wait_send())
        others(NXY, me_xy, lambda j: xy_copy(k, j, xy_dev(j)).wait_send())
        others(NXY, me_xy, lambda j: ga_copy(k, j, xy_dev(j)).wait_send())
        others(NZZ, me_z, lambda j: z_copy(k, j, z_dev(j)).wait_send())
        c_copy(k).wait_send()

    def all_finish(k):
        cg_copy(k, core).wait_send()
        cg_copy(k, 1 - core).wait_recv()

    sides(him, 0, 0)
    acc[...] = jnp.zeros((9 * C, 3 * C), F32)

    def shifted(im, zi, dzs):
        return jnp.concatenate(
            [
                im[zi + 1 - dz, C : 2 * C, NY * (2 - dx) : NY * (2 - dx) + L]
                for dz in dzs
                for dx in range(3)
            ],
            axis=0,
        )

    def pair(im, zi):
        return jnp.concatenate([shifted(im, zi, range(3)), shifted(im, zi + 1, range(3))], axis=1)

    def grad_two(i, carry):
        zi = 2 * i
        acc[...] += dot_nt(pair(gim, zi + 1), jnp.concatenate([him[zi], him[zi + 1]], axis=1))
        return carry

    lax.fori_loop(0, NZ // 2, grad_two, 0)
    pack(0, slopes)
    core_start(0)

    slope, slope_dot = st_finish(1)
    core_finish(0)
    scale = gain * inv_std

    def before(zi, carry):
        for xb in range(NX):
            at = slice(NY * xb, NY * (xb + 1))
            gp = scale * (gh[zi, :, at] - slope - pre[zi, :, at] * slope_dot)
            pim[zi, C : 2 * C, NY * (xb + 1) : NY * (xb + 2)] = gp.astype(BF16)
        return carry

    lax.fori_loop(1, NZ + 1, before, 0)
    halo_start(*p_halo)

    acc[...] = jnp.zeros((9 * C, 3 * C), F32)

    def grad_one(i, carry):
        zi = 2 * i + 1
        at = slice(NY, NY + L)
        acc[...] += dot_nt(pair(pim, zi), jnp.concatenate([xim[zi, :, at], xim[zi + 1, :, at]], axis=1))
        return carry

    lax.fori_loop(0, NZ // 2, grad_one, 0)
    acc[0 : 3 * C] += dot_nt(shifted(pim, 0, (0,)), xim[0, :, NY : NY + L])
    acc[6 * C : 9 * C] += dot_nt(shifted(pim, NZ + 1, (2,)), xim[NZ + 1, :, NY : NY + L])
    pack(1, jnp.zeros((8, NY), F32))
    core_start(1)

    sides(pim, 1, NY)
    core_finish(1)
    conv_inner(pim, w1f, gh)
    xy_finish(0)
    xy_finish(1)
    halo_wait(*p_halo)

    face_planes(hp, pim)
    conv_faces(pim, w1f, gh)

    def finish(zi, carry):
        for xb in range(NX):
            v = gh[zi, :, NY * xb : NY * (xb + 1)]
            up = gim[zi, C : 2 * C, NY * (xb + 1) : NY * (xb + 2)]
            tmp[pl.ds(xb, C, stride=NX), :] = v + up.astype(F32)
        out_ref[:, pl.ds(zi - 1, 1)] = tmp[...].reshape(C, 1, NX, NY).astype(BF16)
        return carry

    lax.fori_loop(1, NZ + 1, finish, 0)
    z_finish(0)
    z_finish(1)
    gather_finish(0)
    all_finish(0)
    separate(total, 0, g2_ref)
    gather_finish(1)
    all_finish(1)
    drain(0)
    drain(1)


def separate(total, k, dst):
    for b in range(9):
        m = total[k, b * C : (b + 1) * C]
        dst[3 * b] = m[:, 0:C]
        dst[3 * b + 1] = m[:, C : 2 * C]
        r, o = (b * C) // 64, (b * C) % 64
        rows = []
        left = C
        while left:
            n = min(64 - o, left)
            rows.append(total[k, 9 * C + o : 9 * C + o + n, 16 * r : 16 * (r + 1)])
            left -= n
            r, o = r + 1, 0
        tail = rows[0] if len(rows) == 1 else jnp.concatenate(rows, axis=0)
        dst[3 * b + 2] = jnp.concatenate([m[:, 2 * C : NY], tail], axis=1)


def results(
    raw, total, g2_raw, out_ref, g1_ref, g2_ref, gain_ref, bias_ref, g1, gain, bias, sem
):
    def copy(i, src, dst):
        each = pltpu.make_async_copy(src, dst, sem.at[i])
        each.start()
        return each

    copies = [copy(0, raw, out_ref), copy(1, g2_raw, g2_ref)]
    bias[...] = total[0, 496:497, 0:C]
    gain[...] = total[0, 497:498, 0:C]
    copies += [copy(2, gain, gain_ref), copy(3, bias, bias_ref)]
    separate(total, 1, g1)
    copies.append(copy(4, g1, g1_ref))
    for each in copies:
        each.wait()


def local(features, upstream, weight_one, weight_two, norm_gain, norm_bias):
    w1 = jnp.transpose(weight_one, (2, 3, 4, 0, 1)).reshape(27, C, C)
    w2 = jnp.transpose(weight_two, (2, 3, 4, 0, 1)).reshape(27, C, C)
    vmem = pl.BlockSpec(memory_space=pltpu.VMEM)
    dma = pltpu.SemaphoreType.DMA
    far = pl.BlockSpec(memory_space=pltpu.HBM)
    raw, total, g2_raw = pl.pallas_call(
        kernel,
        out_shape=(
            pltpu.VMEM((C, NZ, NX, NY), BF16),
            pltpu.VMEM((2, ROWS, NY), F32),
            pltpu.VMEM((27, C, C), F32),
        ),
        in_specs=[far] * 6,
        out_specs=(vmem,) * 3,
        scratch_shapes=[
            pltpu.VMEM((C, NZ, NX, NY), BF16),
            pltpu.VMEM((C, NZ, NX, NY), BF16),
            pltpu.VMEM((27, C, C), BF16),
            pltpu.VMEM((27, C, C), BF16),
            pltpu.VMEM((1, C), F32),
            pltpu.VMEM((1, C), F32),
            dma((6,)),
            pltpu.VMEM((NZ + 2, 3 * C, LP), BF16),
            pltpu.VMEM((NZ + 2, 3 * C, LP), BF16),
            pltpu.VMEM((NZ, 3 * C, L), BF16),
            pltpu.VMEM((NZ + 2, 3 * C, LP), BF16),
            pltpu.VMEM((NZ + 2, C, L), F32),
            pltpu.VMEM((NZ + 2, C, L), F32),
            pltpu.VMEM((C * NX, NY), F32),
            pltpu.VMEM((2, C, L), BF16),
            pltpu.VMEM((2, C, L), BF16),
            pltpu.VMEM((2, C, L), BF16),
            pltpu.VMEM((3 * C, 9 * C), BF16),
            pltpu.VMEM((3 * C, 9 * C), BF16),
            pltpu.VMEM((3 * C, 9 * C), BF16),
            pltpu.VMEM((2, NSP, 8, NY), F32),
            pltpu.VMEM((9 * C, 3 * C), F32),
            pltpu.VMEM((2, ROWS, NY), F32),
            pltpu.VMEM((2, HALF, NY), F32),
            pltpu.VMEM((2, HALF, NY), F32),
            pltpu.VMEM((2, NXY, PIECE, NY), F32),
            pltpu.VMEM((2, NZZ, PIECE, NY), F32),
            dma((3, 2)), dma((3, 2)),
            dma((2, NSP)), dma((2, NSP)),
            dma((2,)), dma((2,)),
            dma((2, NXY)), dma((2, NXY)),
            dma((2, NZZ)), dma((2, NZZ)),
            dma((2, NXY)), dma((2, NXY)),
            dma((2,)), dma((2,)),
        ],
        compiler_params=pltpu.CompilerParams(
            collective_id=0, has_side_effects=True, vmem_limit_bytes=56 * 1024 * 1024
        ),
    )(
        features.reshape(C, NZ, NX, NY),
        upstream.reshape(C, NZ, NX, NY),
        w1,
        w2,
        norm_gain.reshape(1, C),
        norm_bias.reshape(1, C),
    )

    out, g1, g2, gain, bias = pl.pallas_call(
        results,
        out_shape=(
            jax.ShapeDtypeStruct((C, NZ, NX, NY), BF16),
            jax.ShapeDtypeStruct((27, C, C), F32),
            jax.ShapeDtypeStruct((27, C, C), F32),
            jax.ShapeDtypeStruct((1, C), F32),
            jax.ShapeDtypeStruct((1, C), F32),
        ),
        in_specs=[vmem] * 3,
        out_specs=(far,) * 5,
        scratch_shapes=[
            pltpu.VMEM((27, C, C), F32),
            pltpu.VMEM((1, C), F32),
            pltpu.VMEM((1, C), F32),
            dma((5,)),
        ],
    )(*(pltpu.with_memory_space_constraint(v, pltpu.VMEM) for v in (raw, total, g2_raw)))

    def grad(m):
        return jnp.transpose(m.reshape(3, 3, 3, C, C), (3, 4, 0, 1, 2))

    return out.reshape(1, C, NZ, NX, NY), grad(g1), grad(g2), gain.reshape(C), bias.reshape(C)


def solution(mesh):
    cells = P("dp", None, "space", None, None)
    return jax.shard_map(
        local,
        mesh=mesh,
        in_specs=(cells, cells, P(), P(), P(), P()),
        out_specs=(cells, P(), P(), P(), P()),
        check_vma=False,
    )
```

```python
import functools

import jax
import jax.numpy as jnp
from jax import lax
from jax.experimental import pallas as pl
from jax.experimental.pallas import tpu as pltpu
from jax.sharding import PartitionSpec as P

MESH = pl.DeviceIdType.MESH
F32 = jnp.float32
BF16 = jnp.bfloat16
C = 48
NZ, NX, NY = 8, 8, 128
CELLS = 64.0 * NX * NY
EPS = 1e-5
L = NX * NY
LP = L + 2 * NY
SZ_HI, SY, SX, SZ_LO = 2, 4, 4, 4
NXY = SX * SY
NZZ = SZ_HI * SZ_LO
NSP = SZ_HI * SY
ROWS = 512
HALF = ROWS // 2
PIECE = HALF // NXY
SPLIT = 9 * C // 2


def dot(a, b):
    return lax.dot_general(a, b, (((1,), (0,)), ((), ())), preferred_element_type=F32)


def dot_nt(a, b):
    return lax.dot_general(a, b, (((1,), (1,)), ((), ())), preferred_element_type=F32)


def kernel(
    x_hbm, g_hbm, w1_hbm, w2_hbm, gain_hbm, bias_hbm,
    out_ref, total, g2_ref,
    x_ref, g_ref, w1_ref, w2_ref, gain_ref, bias_ref, load,
    xim, gim, him, pim, pre, gh, tmp, hx, hg, hp, w1c, w2f, w1f,
    st, cols, acc, part, core_in, half_sum, xy_in, z_in,
    halo_send, halo_recv, st_send, st_recv, c_send, c_recv, xy_send, xy_recv, z_send, z_recv,
    ga_send, ga_recv, cg_send, cg_recv,
):
    sp = lax.axis_index("space")
    dp = lax.axis_index("dp")
    z_hi, y = sp // SY, sp % SY
    xx_, z_lo, core = dp // (SZ_LO * 2), (dp // 2) % SZ_LO, dp % 2
    me_xy = xx_ * SY + y
    me_z = z_hi * SZ_LO + z_lo
    sibling = (sp, dp + 1 - 2 * core)

    def sp_dev(j):
        return (j, dp)

    def xy_dev(j):
        return (z_hi * SY + j % SY, (j // SY) * (SZ_LO * 2) + z_lo * 2 + core)

    def z_dev(j):
        return ((j // SZ_LO) * SY + y, xx_ * (SZ_LO * 2) + (j % SZ_LO) * 2 + core)

    def others(count, me, body):
        def step(k, carry):
            body(lax.rem(me + k, count))
            return carry
        lax.fori_loop(1, count, step, 0)

    ys = [(y + o) % SY for o in range(SY)]
    xs = [(xx_ + o) % SX for o in range(SX)]
    hops = (0, 1, 2, 1)
    offsets = sorted(((a, b) for a in range(SX) for b in range(SY)), key=lambda o: -hops[o[0]] - hops[o[1]])
    xy_peers = [
        (xs[a] * SY + ys[b], (z_hi * SY + ys[b], xs[a] * (SZ_LO * 2) + z_lo * 2 + core))
        for a, b in offsets[:-1]
    ]
    sp_peers = [
        (side * SY + ys[b], (side * SY + ys[b], dp))
        for side, bs in ((1 - z_hi, (2, 1, 3, 0)), (z_hi, (2, 1, 3)))
        for b in bs
    ]
    z_ids = [(me_z + o) % NZZ for o in (4, 3, 5, 2, 6, 1, 7)]
    z_peers = [(j, z_dev(j)) for j in z_ids]

    loads = [
        pltpu.make_async_copy(src, dst, load.at[i])
        for i, (src, dst) in enumerate(
            ((x_hbm, x_ref), (w1_hbm, w1_ref), (w2_hbm, w2_ref), (g_hbm, g_ref), (gain_hbm, gain_ref), (bias_hbm, bias_ref))
        )
    ]
    for each in loads:
        each.start()

    barrier = pltpu.get_barrier_semaphore()

    def greet(dev):
        pl.semaphore_signal(barrier, inc=1, device_id=dev, device_id_type=MESH)

    for _, dev in sp_peers + z_peers + xy_peers:
        greet(dev)
    greet(sibling)

    lane = lax.broadcasted_iota(jnp.int32, (C, NY), 1)
    eye = lax.broadcasted_iota(jnp.int32, (C, NY), 0) == lane
    first, last = lane == 0, lane == NY - 1

    def column(row):
        return jnp.sum(jnp.where(eye, jnp.broadcast_to(row, (C, NY)), 0.0), axis=1, keepdims=True)

    def as_row(col):
        return jnp.sum(jnp.where(eye, jnp.broadcast_to(col, (C, NY)), 0.0), axis=0, keepdims=True)

    def put_sides(im, zi, at, v):
        im[zi, 0:C, at] = jnp.where(first, 0.0, pltpu.roll(v, 1, 1)).astype(BF16)
        im[zi, 2 * C : 3 * C, at] = jnp.where(last, 0.0, pltpu.roll(v, NY - 1, 1)).astype(BF16)

    def put(im, zi, lo, v):
        at = pl.ds(lo, NY)
        im[zi, C : 2 * C, at] = v.astype(BF16)
        put_sides(im, zi, at, v)

    def sides(im, begin, lo):
        def step(zi, carry):
            for xb in range(NX):
                at = pl.ds(lo + NY * xb, NY)
                put_sides(im, zi, at, im[zi, C : 2 * C, at].astype(F32))
            return carry
        lax.fori_loop(begin, begin + NZ, step, 0)

    def unpack(raw, im, zi):
        tmp[...] = raw.astype(F32).reshape(C * NX, NY)
        for xb in range(NX):
            put(im, zi, NY * (xb + 1), tmp[pl.ds(xb, C, stride=NX), :])

    edge = jnp.zeros((3 * C, NY), BF16)

    def zero_edges(zi, carry):
        for im in (xim, gim, pim):
            im[zi, :, 0:NY] = edge
            im[zi, :, LP - NY : LP] = edge
        return carry

    lax.fori_loop(0, NZ + 2, zero_edges, 0)
    pim[0, C : 2 * C, :] = jnp.zeros((C, LP), BF16)
    pim[NZ + 1, C : 2 * C, :] = jnp.zeros((C, LP), BF16)

    def unpack_own(src, im):
        def step(zi, carry):
            unpack(src[:, pl.ds(zi, 1)].reshape(C, NX, NY), im, zi + 1)
            return carry
        lax.fori_loop(0, NZ, step, 0)

    loads[0].wait()
    unpack_own(x_ref, xim)

    loads[1].wait()
    loads[2].wait()
    for dz in range(3):
        rows = slice(dz * C, (dz + 1) * C)
        blocks = [w1_ref[dz * 9 + t].astype(F32).T for t in range(9)]
        w1c[rows, :] = jnp.concatenate(blocks, axis=0).T.astype(BF16)
        for w_ref, dst in ((w2_ref, w2f), (w1_ref, w1f)):
            blocks = [w_ref[26 - (dz * 9 + t)].astype(F32) for t in range(9)]
            dst[rows, :] = jnp.concatenate(blocks, axis=0).T.astype(BF16)

    has_up, has_down = sp < NSP - 1, sp > 0

    def halo_copy(src, dst, k, slot, dev):
        return pltpu.make_async_remote_copy(
            src_ref=src, dst_ref=dst.at[slot], send_sem=halo_send.at[k, slot],
            recv_sem=halo_recv.at[k, slot], device_id=dev, device_id_type=MESH,
        )

    def halo_start(low, high, dst, k):
        @pl.when(has_up)
        def _():
            halo_copy(high, dst, k, 0, (sp + 1, dp)).start()

        @pl.when(has_down)
        def _():
            halo_copy(low, dst, k, 1, (sp - 1, dp)).start()

    def halo_wait(low, high, dst, k):
        @pl.when(has_up)
        def _():
            halo_copy(high, dst, k, 0, (sp + 1, dp)).wait_send()
            halo_copy(high, dst, k, 1, (sp + 1, dp)).wait_recv()

        @pl.when(has_down)
        def _():
            halo_copy(low, dst, k, 1, (sp - 1, dp)).wait_send()
            halo_copy(low, dst, k, 0, (sp - 1, dp)).wait_recv()

    def halo_of(im, dst, k):
        at = (slice(C, 2 * C), slice(NY, NY + L))
        return im.at[(1,) + at], im.at[(NZ,) + at], dst, k

    x_halo = halo_of(xim, hx, 0)
    g_halo = halo_of(gim, hg, 1)
    p_halo = halo_of(pim, hp, 2)

    def window(im, zi):
        return jnp.concatenate([im[zi, :, NY * d : NY * d + L] for d in range(3)], axis=0)

    def conv_inner(im, w, dst):
        dst[0] = jnp.zeros((C, L), F32)
        dst[1] = jnp.zeros((C, L), F32)

        def step(zi, carry):
            p = dot(w[...], window(im, zi))
            dst[zi + 1] = p[0:C]
            dst[zi] += p[C : 2 * C]
            dst[zi - 1] += p[2 * C : 3 * C]
            return carry

        lax.fori_loop(1, NZ + 1, step, 0)

    def conv_faces(im, w, dst):
        dst[1] += dot(w[0:C], window(im, 0))
        dst[NZ] += dot(w[2 * C : 3 * C], window(im, NZ + 1))

    def face_planes(dst, im):
        for slot, zi, live in ((0, 0, has_down), (1, NZ + 1, has_up)):
            for xb in range(NX):
                v = dst[slot, :, NY * xb : NY * (xb + 1)].astype(F32)
                put(im, zi, NY * (xb + 1), jnp.where(live, v, 0.0))

    def st_copy(k, j, dev):
        return pltpu.make_async_remote_copy(
            src_ref=st.at[k, sp], dst_ref=st.at[k, sp], send_sem=st_send.at[k, j],
            recv_sem=st_recv.at[k, sp], device_id=dev, device_id_type=MESH,
        )

    def st_wait(k, j):
        return pltpu.make_async_remote_copy(
            src_ref=st.at[k, j], dst_ref=st.at[k, j], send_sem=st_send.at[k, j],
            recv_sem=st_recv.at[k, j], device_id=sp_dev(j), device_id_type=MESH,
        )

    def st_start(k, one, two):
        row_one = as_row(jnp.sum(one, axis=1, keepdims=True))
        row_two = as_row(jnp.sum(two, axis=1, keepdims=True))
        lead = lax.broadcasted_iota(jnp.int32, (8, NY), 0)
        mine = jnp.where(lead == 0, row_one, 0.0) + jnp.where(lead == 1, row_two, 0.0)
        st[k, sp] = mine
        for j, dev in sp_peers:
            st_copy(k, j, dev).start()
        return mine

    def st_finish(k):
        others(NSP, sp, lambda j: st_wait(k, j).wait_recv())
        s = st[k, 0]
        for j in range(1, NSP):
            s = s + st[k, j]
        return column(s[0:1] / CELLS), column(s[1:2] / CELLS)

    conv_inner(xim, w1c, pre)
    pl.semaphore_wait(barrier, 1 + (NSP - 1) + (NXY - 1) + (NZZ - 1))

    halo_start(*x_halo)
    loads[3].wait()
    unpack_own(g_ref, gim)
    halo_start(*g_halo)
    conv_inner(gim, w2f, gh)

    zero = jnp.zeros((C, NY), F32)

    def moments(zi, carry):
        one, two = carry
        for xb in range(NX):
            v = pre[zi, :, NY * xb : NY * (xb + 1)]
            one, two = one + v, two + v * v
        return one, two

    sums = lax.fori_loop(2, NZ, moments, (zero, zero))
    halo_wait(*x_halo)
    face_planes(hx, xim)
    conv_faces(xim, w1c, pre)
    st_start(0, *moments(NZ, moments(1, sums)))

    halo_wait(*g_halo)
    face_planes(hg, gim)
    conv_faces(gim, w2f, gh)

    loads[4].wait()
    loads[5].wait()
    pad = jnp.zeros((1, NY - C), F32)
    def spread(i, col):
        cols[i] = jnp.broadcast_to(col, (C, NY))

    gain = column(jnp.concatenate([gain_ref[...], pad], axis=1))
    spread(2, gain)
    spread(3, column(jnp.concatenate([bias_ref[...], pad], axis=1)))
    mean, square = st_finish(0)
    inv_std = lax.rsqrt(square - mean * mean + EPS)
    spread(0, mean)
    spread(1, inv_std)

    def activate(zi, carry):
        one, two = carry
        for xb in range(NX):
            at = slice(NY * xb, NY * (xb + 1))
            hat = (pre[zi, :, at] - cols[0]) * cols[1]
            normed = hat * cols[2] + cols[3]
            sig = jax.nn.sigmoid(normed)
            act = normed * sig
            him[zi - 1, C : 2 * C, at] = act.astype(BF16)
            gn = gh[zi, :, at] * (sig + act * (1.0 - sig))
            gh[zi, :, at] = gn
            pre[zi, :, at] = hat
            one, two = one + gn, two + gn * hat
        return one, two

    slopes = st_start(1, *lax.fori_loop(1, NZ + 1, activate, (zero, zero)))

    def c_copy(k):
        return pltpu.make_async_remote_copy(
            src_ref=part.at[k, pl.ds((1 - core) * HALF, HALF)], dst_ref=core_in.at[k],
            send_sem=c_send.at[k], recv_sem=c_recv.at[k], device_id=sibling, device_id_type=MESH,
        )

    def pack(k, p, v, tail):
        base = p * HALF
        part[k, pl.ds(base, SPLIT)] = v[:, 0:NY]
        rest = jnp.concatenate([v[:, NY : NY + 16], jnp.zeros((256 - SPLIT, 16), F32)], axis=0)
        pieces = [rest[32 * r : 32 * (r + 1)] for r in range(8)]
        part[k, pl.ds(base + SPLIT, 32)] = jnp.concatenate(pieces, axis=1)
        part[k, pl.ds(base + SPLIT + 32, 8)] = tail

    def core_start(k):
        c_copy(k).start()

    def xy_copy(k, j, dev):
        return pltpu.make_async_remote_copy(
            src_ref=half_sum.at[k, pl.ds(j * PIECE, PIECE)], dst_ref=xy_in.at[k, me_xy],
            send_sem=xy_send.at[k, j], recv_sem=xy_recv.at[k, me_xy], device_id=dev, device_id_type=MESH,
        )

    def xy_wait(k, j):
        return pltpu.make_async_remote_copy(
            src_ref=xy_in.at[k, j], dst_ref=xy_in.at[k, j],
            send_sem=xy_send.at[k, j], recv_sem=xy_recv.at[k, j], device_id=xy_dev(j), device_id_type=MESH,
        )

    def core_finish(k):
        c_copy(k).wait_recv()
        half_sum[k] = part[k, pl.ds(core * HALF, HALF)] + core_in[k]
        for j, dev in xy_peers:
            xy_copy(k, j, dev).start()

    def z_copy(k, j, dev):
        return pltpu.make_async_remote_copy(
            src_ref=z_in.at[k, me_z], dst_ref=z_in.at[k, me_z],
            send_sem=z_send.at[k, j], recv_sem=z_recv.at[k, me_z], device_id=dev, device_id_type=MESH,
        )

    def z_wait(k, j):
        return pltpu.make_async_remote_copy(
            src_ref=z_in.at[k, j], dst_ref=z_in.at[k, j],
            send_sem=z_send.at[k, j], recv_sem=z_recv.at[k, j], device_id=z_dev(j), device_id_type=MESH,
        )

    def xy_finish(k):
        others(NXY, me_xy, lambda j: xy_wait(k, j).wait_recv())
        xy_in[k, me_xy] = half_sum[k, pl.ds(me_xy * PIECE, PIECE)]
        s = xy_in[k, 0]
        for j in range(1, NXY):
            s = s + xy_in[k, j]
        z_in[k, me_z] = s
        for j, dev in z_peers:
            z_copy(k, j, dev).start()

    def ga_at(j):
        return pl.ds(core * HALF + j * PIECE, PIECE)

    def ga_copy(k, j, dev):
        return pltpu.make_async_remote_copy(
            src_ref=total.at[k, ga_at(me_xy)], dst_ref=total.at[k, ga_at(me_xy)],
            send_sem=ga_send.at[k, j], recv_sem=ga_recv.at[k, me_xy], device_id=dev, device_id_type=MESH,
        )

    def ga_wait(k, j):
        return pltpu.make_async_remote_copy(
            src_ref=total.at[k, ga_at(j)], dst_ref=total.at[k, ga_at(j)],
            send_sem=ga_send.at[k, j], recv_sem=ga_recv.at[k, j], device_id=xy_dev(j), device_id_type=MESH,
        )

    def z_finish(k):
        others(NZZ, me_z, lambda j: z_wait(k, j).wait_recv())
        s = z_in[k, 0]
        for j in range(1, NZZ):
            s = s + z_in[k, j]
        total[k, ga_at(me_xy)] = s
        cg_copy(k, core, me_xy).start()
        for j, dev in xy_peers:
            ga_copy(k, j, dev).start()

    def cg_copy(k, which, j):
        at = pl.ds(which * HALF + j * PIECE, PIECE)
        return pltpu.make_async_remote_copy(
            src_ref=total.at[k, at], dst_ref=total.at[k, at],
            send_sem=cg_send.at[k, j], recv_sem=cg_recv.at[k, j], device_id=sibling, device_id_type=MESH,
        )

    def gather_finish(k):
        for j, _ in reversed(xy_peers):
            ga_wait(k, j).wait_recv()
            cg_copy(k, core, j).start()

    def drain(k):
        others(NSP, sp, lambda j: st_copy(k, j, sp_dev(j)).wait_send())
        others(NXY, me_xy, lambda j: xy_copy(k, j, xy_dev(j)).wait_send())
        others(NXY, me_xy, lambda j: ga_copy(k, j, xy_dev(j)).wait_send())
        others(NZZ, me_z, lambda j: z_copy(k, j, z_dev(j)).wait_send())
        c_copy(k).wait_send()
        all_sent(k)

    def all_finish(k):
        def step(j, carry):
            cg_copy(k, 1 - core, j).wait_recv()
            return carry
        lax.fori_loop(0, NXY, step, 0)

    def all_sent(k):
        def step(j, carry):
            cg_copy(k, core, j).wait_send()
            return carry
        lax.fori_loop(0, NXY, step, 0)

    sides(him, 0, 0)
    lhs = jnp.concatenate(
        [
            jnp.concatenate(
                [
                    gim[zi + 1 - dz, C : 2 * C, NY * (2 - dx) : NY * (2 - dx) + L]
                    for dz in range(3)
                    for dx in range(3)
                ],
                axis=0,
            )
            for zi in range(1, NZ + 1)
        ],
        axis=1,
    )
    acc[...] = dot_nt(lhs, jnp.concatenate([him[zi] for zi in range(NZ)], axis=1))
    pack(0, 0, acc[0:SPLIT], slopes)
    pack(0, 1, acc[SPLIT : 2 * SPLIT], jnp.zeros((8, NY), F32))
    core_start(0)
    core_finish(0)

    slope, slope_dot = st_finish(1)
    spread(4, gain * inv_std)
    spread(5, slope)
    spread(6, slope_dot)

    def before(zi, carry):
        for xb in range(NX):
            at = slice(NY * xb, NY * (xb + 1))
            gp = cols[4] * (gh[zi, :, at] - cols[5] - pre[zi, :, at] * cols[6])
            pim[zi, C : 2 * C, NY * (xb + 1) : NY * (xb + 2)] = gp.astype(BF16)
        return carry

    lax.fori_loop(1, NZ + 1, before, 0)
    halo_start(*p_halo)

    def grad_one(p):
        def block(zi, i):
            b = 4 * p + i
            dz, dx = b // 3, b % 3
            return pim[zi + 1 - dz, C : 2 * C, pl.ds(pl.multiple_of(NY * (2 - dx), NY), L)]

        lhs = jnp.concatenate(
            [
                jnp.concatenate([block(zi, i) for i in range(5)], axis=0)
                for zi in range(1, NZ + 1)
            ],
            axis=1,
        )
        inner = slice(NY, NY + L)
        rhs = jnp.concatenate([xim[zi, :, inner] for zi in range(1, NZ + 1)], axis=1)
        acc[0 : 5 * C] = dot_nt(lhs, rhs)
        face = jnp.concatenate(
            [pim[1 + (NZ - 1) * p, C : 2 * C, NY * (2 - dx) : NY * (2 - dx) + L] for dx in range(3)], axis=0
        )
        rows = pl.ds(pl.multiple_of(2 * C * p, 8), 3 * C)
        acc[rows] += dot_nt(face, xim[(NZ + 1) * p, :, inner])
        pack(1, p, acc[pl.ds(pl.multiple_of((C // 2) * p, 8), SPLIT)], jnp.zeros((8, NY), F32))

    grad_one(1 - core)
    core_start(1)
    grad_one(core)
    core_finish(1)

    xy_finish(0)
    sides(pim, 1, NY)
    conv_inner(pim, w1f, gh)
    z_finish(0)
    xy_finish(1)
    halo_wait(*p_halo)

    face_planes(hp, pim)
    conv_faces(pim, w1f, gh)

    def finish(zi, carry):
        for xb in range(NX):
            v = gh[zi, :, NY * xb : NY * (xb + 1)]
            up = gim[zi, C : 2 * C, NY * (xb + 1) : NY * (xb + 2)]
            tmp[pl.ds(xb, C, stride=NX), :] = v + up.astype(F32)
        out_ref[:, pl.ds(zi - 1, 1)] = tmp[...].reshape(C, 1, NX, NY).astype(BF16)
        return carry

    lax.fori_loop(1, NZ + 1, finish, 0)
    gather_finish(0)
    z_finish(1)
    all_finish(0)
    separate(total, 0, g2_ref)
    gather_finish(1)
    drain(0)
    all_finish(1)
    drain(1)


def separate(total, k, dst, done=None):
    main, tail = [], []
    for p in range(2):
        base = p * HALF
        rest = [total[k, base + SPLIT : base + SPLIT + 32, 16 * r : 16 * (r + 1)] for r in range(7)]
        rest[6] = rest[6][0 : SPLIT - 192]
        main.append(total[k, base : base + SPLIT])
        tail.append(jnp.concatenate(rest, axis=0))
    main, tail = jnp.concatenate(main, axis=0), jnp.concatenate(tail, axis=0)
    for b in range(9):
        rows = slice(b * C, (b + 1) * C)
        m = main[rows]
        dst[3 * b] = m[:, 0:C]
        dst[3 * b + 1] = m[:, C : 2 * C]
        dst[3 * b + 2] = jnp.concatenate([m[:, 2 * C : NY], tail[rows]], axis=1)
        if done is not None and b % 3 == 2:
            done(b // 3)


def results(
    raw, total, g2_raw, out_ref, g1_ref, g2_ref, gain_ref, bias_ref, g1, gain, bias, sem
):
    def copy(i, src, dst):
        each = pltpu.make_async_copy(src, dst, sem.at[i])
        each.start()
        return each

    copies = [copy(0, raw, out_ref), copy(1, g2_raw, g2_ref)]
    row = SPLIT + 32
    bias[...] = total[0, row : row + 1, 0:C]
    gain[...] = total[0, row + 1 : row + 2, 0:C]
    copies += [copy(2, gain, gain_ref), copy(3, bias, bias_ref)]

    def send(third):
        at = pl.ds(9 * third, 9)
        copies.append(copy(4 + third, g1.at[at], g1_ref.at[at]))

    separate(total, 1, g1, send)
    for each in copies:
        each.wait()


def local(features, upstream, weight_one, weight_two, norm_gain, norm_bias):
    w1 = jnp.transpose(weight_one, (2, 3, 4, 0, 1)).reshape(27, C, C)
    w2 = jnp.transpose(weight_two, (2, 3, 4, 0, 1)).reshape(27, C, C)
    vmem = pl.BlockSpec(memory_space=pltpu.VMEM)
    dma = pltpu.SemaphoreType.DMA
    far = pl.BlockSpec(memory_space=pltpu.HBM)
    raw, total, g2_raw = pl.pallas_call(
        kernel,
        out_shape=(
            pltpu.VMEM((C, NZ, NX, NY), BF16),
            pltpu.VMEM((2, ROWS, NY), F32),
            pltpu.VMEM((27, C, C), F32),
        ),
        in_specs=[far] * 6,
        out_specs=(vmem,) * 3,
        scratch_shapes=[
            pltpu.VMEM((C, NZ, NX, NY), BF16),
            pltpu.VMEM((C, NZ, NX, NY), BF16),
            pltpu.VMEM((27, C, C), BF16),
            pltpu.VMEM((27, C, C), BF16),
            pltpu.VMEM((1, C), F32),
            pltpu.VMEM((1, C), F32),
            dma((6,)),
            pltpu.VMEM((NZ + 2, 3 * C, LP), BF16),
            pltpu.VMEM((NZ + 2, 3 * C, LP), BF16),
            pltpu.VMEM((NZ, 3 * C, L), BF16),
            pltpu.VMEM((NZ + 2, 3 * C, LP), BF16),
            pltpu.VMEM((NZ + 2, C, L), F32),
            pltpu.VMEM((NZ + 2, C, L), F32),
            pltpu.VMEM((C * NX, NY), F32),
            pltpu.VMEM((2, C, L), BF16),
            pltpu.VMEM((2, C, L), BF16),
            pltpu.VMEM((2, C, L), BF16),
            pltpu.VMEM((3 * C, 9 * C), BF16),
            pltpu.VMEM((3 * C, 9 * C), BF16),
            pltpu.VMEM((3 * C, 9 * C), BF16),
            pltpu.VMEM((2, NSP, 8, NY), F32),
            pltpu.VMEM((7, C, NY), F32),
            pltpu.VMEM((9 * C, 3 * C), F32),
            pltpu.VMEM((2, ROWS, NY), F32),
            pltpu.VMEM((2, HALF, NY), F32),
            pltpu.VMEM((2, HALF, NY), F32),
            pltpu.VMEM((2, NXY, PIECE, NY), F32),
            pltpu.VMEM((2, NZZ, PIECE, NY), F32),
            dma((3, 2)), dma((3, 2)),
            dma((2, NSP)), dma((2, NSP)),
            dma((2,)), dma((2,)),
            dma((2, NXY)), dma((2, NXY)),
            dma((2, NZZ)), dma((2, NZZ)),
            dma((2, NXY)), dma((2, NXY)),
            dma((2, NXY)), dma((2, NXY)),
        ],
        compiler_params=pltpu.CompilerParams(
            collective_id=0, has_side_effects=True, vmem_limit_bytes=56 * 1024 * 1024
        ),
    )(
        features.reshape(C, NZ, NX, NY),
        upstream.reshape(C, NZ, NX, NY),
        w1,
        w2,
        norm_gain.reshape(1, C),
        norm_bias.reshape(1, C),
    )

    out, g1, g2, gain, bias = pl.pallas_call(
        results,
        out_shape=(
            jax.ShapeDtypeStruct((C, NZ, NX, NY), BF16),
            jax.ShapeDtypeStruct((27, C, C), F32),
            jax.ShapeDtypeStruct((27, C, C), F32),
            jax.ShapeDtypeStruct((1, C), F32),
            jax.ShapeDtypeStruct((1, C), F32),
        ),
        in_specs=[vmem] * 3,
        out_specs=(far,) * 5,
        scratch_shapes=[
            pltpu.VMEM((27, C, C), F32),
            pltpu.VMEM((1, C), F32),
            pltpu.VMEM((1, C), F32),
            dma((7,)),
        ],
    )(*(pltpu.with_memory_space_constraint(v, pltpu.VMEM) for v in (raw, total, g2_raw)))

    def grad(m):
        return jnp.transpose(m.reshape(3, 3, 3, C, C), (3, 4, 0, 1, 2))

    return out.reshape(1, C, NZ, NX, NY), grad(g1), grad(g2), gain.reshape(C), bias.reshape(C)


def solution(mesh):
    cells = P("dp", None, "space", None, None)
    return jax.shard_map(
        local,
        mesh=mesh,
        in_specs=(cells, cells, P(), P(), P(), P()),
        out_specs=(cells, P(), P(), P(), P()),
        check_vma=False,
    )
```

```python
import functools

import jax
import jax.numpy as jnp
from jax import lax
from jax.experimental import pallas as pl
from jax.experimental.pallas import tpu as pltpu
from jax.sharding import PartitionSpec as P

MESH = pl.DeviceIdType.MESH
F32 = jnp.float32
BF16 = jnp.bfloat16
C = 48
NZ, NX, NY = 8, 8, 128
CELLS = 64.0 * NX * NY
EPS = 1e-5
L = NX * NY
LP = L + 2 * NY
SZ_HI, SY, SX, SZ_LO = 2, 4, 4, 4
NXY = SX * SY
NZZ = SZ_HI * SZ_LO
NSP = SZ_HI * SY
ROWS = 512
HALF = ROWS // 2
PIECE = HALF // NXY
SPLIT = 9 * C // 2


def dot(a, b):
    return lax.dot_general(a, b, (((1,), (0,)), ((), ())), preferred_element_type=F32)


def dot_nt(a, b):
    return lax.dot_general(a, b, (((1,), (1,)), ((), ())), preferred_element_type=F32)


def kernel(
    x_hbm, g_hbm, w1_hbm, w2_hbm, gain_hbm, bias_hbm,
    out_ref, total, g2_ref,
    x_ref, g_ref, w1_ref, w2_ref, gain_ref, bias_ref, load,
    xim, gim, him, pim, pre, gh, tmp, hx, hg, hp, w1c, w2f, w1f,
    st, cols, acc, part, core_in, half_sum, xy_in, z_in,
    halo_send, halo_recv, st_send, st_recv, c_send, c_recv, xy_send, xy_recv, z_send, z_recv,
    ga_send, ga_recv, cg_send, cg_recv,
):
    sp = lax.axis_index("space")
    dp = lax.axis_index("dp")
    z_hi, y = sp // SY, sp % SY
    xx_, z_lo, core = dp // (SZ_LO * 2), (dp // 2) % SZ_LO, dp % 2
    me_xy = xx_ * SY + y
    me_z = z_hi * SZ_LO + z_lo
    sibling = (sp, dp + 1 - 2 * core)

    def sp_dev(j):
        return (j, dp)

    def xy_dev(j):
        return (z_hi * SY + j % SY, (j // SY) * (SZ_LO * 2) + z_lo * 2 + core)

    def z_dev(j):
        return ((j // SZ_LO) * SY + y, xx_ * (SZ_LO * 2) + (j % SZ_LO) * 2 + core)

    def others(count, me, body):
        def step(k, carry):
            body(lax.rem(me + k, count))
            return carry
        lax.fori_loop(1, count, step, 0)

    ys = [(y + o) % SY for o in range(SY)]
    xs = [(xx_ + o) % SX for o in range(SX)]
    hops = (0, 1, 2, 1)
    offsets = sorted(((a, b) for a in range(SX) for b in range(SY)), key=lambda o: -hops[o[0]] - hops[o[1]])
    xy_peers = [
        (xs[a] * SY + ys[b], (z_hi * SY + ys[b], xs[a] * (SZ_LO * 2) + z_lo * 2 + core))
        for a, b in offsets[:-1]
    ]
    sp_peers = [
        (side * SY + ys[b], (side * SY + ys[b], dp))
        for side, bs in ((1 - z_hi, (2, 1, 3, 0)), (z_hi, (2, 1, 3)))
        for b in bs
    ]
    z_ids = [(me_z + o) % NZZ for o in (4, 3, 5, 2, 6, 1, 7)]
    z_peers = [(j, z_dev(j)) for j in z_ids]

    loads = [
        pltpu.make_async_copy(src, dst, load.at[i])
        for i, (src, dst) in enumerate(
            ((x_hbm, x_ref), (w1_hbm, w1_ref), (w2_hbm, w2_ref), (g_hbm, g_ref), (gain_hbm, gain_ref), (bias_hbm, bias_ref))
        )
    ]
    for each in loads:
        each.start()

    barrier = pltpu.get_barrier_semaphore()

    def greet(dev):
        pl.semaphore_signal(barrier, inc=1, device_id=dev, device_id_type=MESH)

    for _, dev in sp_peers + z_peers + xy_peers:
        greet(dev)
    greet(sibling)

    lane = lax.broadcasted_iota(jnp.int32, (C, NY), 1)
    eye = lax.broadcasted_iota(jnp.int32, (C, NY), 0) == lane
    first, last = lane == 0, lane == NY - 1

    def column(row):
        return jnp.sum(jnp.where(eye, jnp.broadcast_to(row, (C, NY)), 0.0), axis=1, keepdims=True)

    def as_row(col):
        return jnp.sum(jnp.where(eye, jnp.broadcast_to(col, (C, NY)), 0.0), axis=0, keepdims=True)

    def put_sides(im, zi, at, v):
        im[zi, 0:C, at] = jnp.where(first, 0.0, pltpu.roll(v, 1, 1)).astype(BF16)
        im[zi, 2 * C : 3 * C, at] = jnp.where(last, 0.0, pltpu.roll(v, NY - 1, 1)).astype(BF16)

    def put(im, zi, lo, v):
        at = pl.ds(lo, NY)
        im[zi, C : 2 * C, at] = v.astype(BF16)
        put_sides(im, zi, at, v)

    def sides(im, begin, lo):
        def step(zi, carry):
            for xb in range(NX):
                at = pl.ds(lo + NY * xb, NY)
                put_sides(im, zi, at, im[zi, C : 2 * C, at].astype(F32))
            return carry
        lax.fori_loop(begin, begin + NZ, step, 0)

    def unpack(raw, im, zi):
        tmp[...] = raw.astype(F32).reshape(C * NX, NY)
        for xb in range(NX):
            put(im, zi, NY * (xb + 1), tmp[pl.ds(xb, C, stride=NX), :])

    edge = jnp.zeros((3 * C, NY), BF16)

    def zero_edges(zi, carry):
        for im in (xim, gim, pim):
            im[zi, :, 0:NY] = edge
            im[zi, :, LP - NY : LP] = edge
        return carry

    lax.fori_loop(0, NZ + 2, zero_edges, 0)
    pim[0, C : 2 * C, :] = jnp.zeros((C, LP), BF16)
    pim[NZ + 1, C : 2 * C, :] = jnp.zeros((C, LP), BF16)

    def unpack_own(src, im):
        def step(zi, carry):
            unpack(src[:, pl.ds(zi, 1)].reshape(C, NX, NY), im, zi + 1)
            return carry
        lax.fori_loop(0, NZ, step, 0)

    loads[0].wait()
    unpack_own(x_ref, xim)

    loads[1].wait()
    loads[2].wait()
    for dz in range(3):
        rows = slice(dz * C, (dz + 1) * C)
        blocks = [w1_ref[dz * 9 + t].astype(F32).T for t in range(9)]
        w1c[rows, :] = jnp.concatenate(blocks, axis=0).T.astype(BF16)
        for w_ref, dst in ((w2_ref, w2f), (w1_ref, w1f)):
            blocks = [w_ref[26 - (dz * 9 + t)].astype(F32) for t in range(9)]
            dst[rows, :] = jnp.concatenate(blocks, axis=0).T.astype(BF16)

    has_up, has_down = sp < NSP - 1, sp > 0

    def halo_copy(src, dst, k, slot, dev):
        return pltpu.make_async_remote_copy(
            src_ref=src, dst_ref=dst.at[slot], send_sem=halo_send.at[k, slot],
            recv_sem=halo_recv.at[k, slot], device_id=dev, device_id_type=MESH,
        )

    def halo_start(low, high, dst, k):
        @pl.when(has_up)
        def _():
            halo_copy(high, dst, k, 0, (sp + 1, dp)).start()

        @pl.when(has_down)
        def _():
            halo_copy(low, dst, k, 1, (sp - 1, dp)).start()

    def halo_wait(low, high, dst, k):
        @pl.when(has_up)
        def _():
            halo_copy(high, dst, k, 0, (sp + 1, dp)).wait_send()
            halo_copy(high, dst, k, 1, (sp + 1, dp)).wait_recv()

        @pl.when(has_down)
        def _():
            halo_copy(low, dst, k, 1, (sp - 1, dp)).wait_send()
            halo_copy(low, dst, k, 0, (sp - 1, dp)).wait_recv()

    def halo_of(im, dst, k):
        at = (slice(C, 2 * C), slice(NY, NY + L))
        return im.at[(1,) + at], im.at[(NZ,) + at], dst, k

    x_halo = halo_of(xim, hx, 0)
    g_halo = halo_of(gim, hg, 1)
    p_halo = halo_of(pim, hp, 2)

    def window(im, zi):
        return jnp.concatenate([im[zi, :, NY * d : NY * d + L] for d in range(3)], axis=0)

    def conv_inner(im, w, dst):
        dst[0] = jnp.zeros((C, L), F32)
        dst[1] = jnp.zeros((C, L), F32)

        def step(zi, carry):
            p = dot(w[...], window(im, zi))
            dst[zi + 1] = p[0:C]
            dst[zi] += p[C : 2 * C]
            dst[zi - 1] += p[2 * C : 3 * C]
            return carry

        lax.fori_loop(1, NZ + 1, step, 0)

    def conv_faces(im, w, dst):
        dst[1] += dot(w[0:C], window(im, 0))
        dst[NZ] += dot(w[2 * C : 3 * C], window(im, NZ + 1))

    def face_planes(dst, im):
        for slot, zi, live in ((0, 0, has_down), (1, NZ + 1, has_up)):
            for xb in range(NX):
                v = dst[slot, :, NY * xb : NY * (xb + 1)].astype(F32)
                put(im, zi, NY * (xb + 1), jnp.where(live, v, 0.0))

    def st_copy(k, j, dev):
        return pltpu.make_async_remote_copy(
            src_ref=st.at[k, sp], dst_ref=st.at[k, sp], send_sem=st_send.at[k, j],
            recv_sem=st_recv.at[k, sp], device_id=dev, device_id_type=MESH,
        )

    def st_wait(k, j):
        return pltpu.make_async_remote_copy(
            src_ref=st.at[k, j], dst_ref=st.at[k, j], send_sem=st_send.at[k, j],
            recv_sem=st_recv.at[k, j], device_id=sp_dev(j), device_id_type=MESH,
        )

    def st_start(k, one, two):
        row_one = as_row(jnp.sum(one, axis=1, keepdims=True))
        row_two = as_row(jnp.sum(two, axis=1, keepdims=True))
        lead = lax.broadcasted_iota(jnp.int32, (8, NY), 0)
        mine = jnp.where(lead == 0, row_one, 0.0) + jnp.where(lead == 1, row_two, 0.0)
        st[k, sp] = mine
        for j, dev in sp_peers:
            st_copy(k, j, dev).start()
        return mine

    def st_finish(k):
        others(NSP, sp, lambda j: st_wait(k, j).wait_recv())
        s = st[k, 0]
        for j in range(1, NSP):
            s = s + st[k, j]
        return column(s[0:1] / CELLS), column(s[1:2] / CELLS)

    conv_inner(xim, w1c, pre)
    pl.semaphore_wait(barrier, 1 + (NSP - 1) + (NXY - 1) + (NZZ - 1))

    halo_start(*x_halo)
    loads[3].wait()
    unpack_own(g_ref, gim)
    conv_inner(gim, w2f, gh)
    halo_start(*g_halo)

    zero = jnp.zeros((C, NY), F32)

    def moments(zi, carry):
        one, two = carry
        for xb in range(NX):
            v = pre[zi, :, NY * xb : NY * (xb + 1)]
            one, two = one + v, two + v * v
        return one, two

    sums = lax.fori_loop(2, NZ, moments, (zero, zero))
    halo_wait(*x_halo)
    face_planes(hx, xim)
    conv_faces(xim, w1c, pre)
    st_start(0, *moments(NZ, moments(1, sums)))

    halo_wait(*g_halo)
    face_planes(hg, gim)
    conv_faces(gim, w2f, gh)

    loads[4].wait()
    loads[5].wait()
    pad = jnp.zeros((1, NY - C), F32)
    def spread(i, col):
        cols[i] = jnp.broadcast_to(col, (C, NY))

    gain = column(jnp.concatenate([gain_ref[...], pad], axis=1))
    spread(2, gain)
    spread(3, column(jnp.concatenate([bias_ref[...], pad], axis=1)))
    mean, square = st_finish(0)
    inv_std = lax.rsqrt(square - mean * mean + EPS)
    spread(0, mean)
    spread(1, inv_std)

    def activate(zi, carry):
        one, two = carry
        for xb in range(NX):
            at = slice(NY * xb, NY * (xb + 1))
            hat = (pre[zi, :, at] - cols[0]) * cols[1]
            normed = hat * cols[2] + cols[3]
            sig = jax.nn.sigmoid(normed)
            act = normed * sig
            him[zi - 1, C : 2 * C, at] = act.astype(BF16)
            gn = gh[zi, :, at] * (sig + act * (1.0 - sig))
            gh[zi, :, at] = gn
            pre[zi, :, at] = hat
            one, two = one + gn, two + gn * hat
        return one, two

    slopes = st_start(1, *lax.fori_loop(1, NZ + 1, activate, (zero, zero)))

    def c_copy(k):
        return pltpu.make_async_remote_copy(
            src_ref=part.at[k, pl.ds((1 - core) * HALF, HALF)], dst_ref=core_in.at[k],
            send_sem=c_send.at[k], recv_sem=c_recv.at[k], device_id=sibling, device_id_type=MESH,
        )

    def pack(k, p, v, tail):
        base = p * HALF
        part[k, pl.ds(base, SPLIT)] = v[:, 0:NY]
        rest = jnp.concatenate([v[:, NY : NY + 16], jnp.zeros((256 - SPLIT, 16), F32)], axis=0)
        pieces = [rest[32 * r : 32 * (r + 1)] for r in range(8)]
        part[k, pl.ds(base + SPLIT, 32)] = jnp.concatenate(pieces, axis=1)
        part[k, pl.ds(base + SPLIT + 32, 8)] = tail

    def core_start(k):
        c_copy(k).start()

    def xy_copy(k, j, dev):
        return pltpu.make_async_remote_copy(
            src_ref=half_sum.at[k, pl.ds(j * PIECE, PIECE)], dst_ref=xy_in.at[k, me_xy],
            send_sem=xy_send.at[k, j], recv_sem=xy_recv.at[k, me_xy], device_id=dev, device_id_type=MESH,
        )

    def xy_wait(k, j):
        return pltpu.make_async_remote_copy(
            src_ref=xy_in.at[k, j], dst_ref=xy_in.at[k, j],
            send_sem=xy_send.at[k, j], recv_sem=xy_recv.at[k, j], device_id=xy_dev(j), device_id_type=MESH,
        )

    def core_finish(k):
        c_copy(k).wait_recv()
        half_sum[k] = part[k, pl.ds(core * HALF, HALF)] + core_in[k]
        for j, dev in xy_peers:
            xy_copy(k, j, dev).start()

    def z_copy(k, j, dev):
        return pltpu.make_async_remote_copy(
            src_ref=z_in.at[k, me_z], dst_ref=z_in.at[k, me_z],
            send_sem=z_send.at[k, j], recv_sem=z_recv.at[k, me_z], device_id=dev, device_id_type=MESH,
        )

    def z_wait(k, j):
        return pltpu.make_async_remote_copy(
            src_ref=z_in.at[k, j], dst_ref=z_in.at[k, j],
            send_sem=z_send.at[k, j], recv_sem=z_recv.at[k, j], device_id=z_dev(j), device_id_type=MESH,
        )

    def xy_finish(k):
        others(NXY, me_xy, lambda j: xy_wait(k, j).wait_recv())
        xy_in[k, me_xy] = half_sum[k, pl.ds(me_xy * PIECE, PIECE)]
        s = xy_in[k, 0]
        for j in range(1, NXY):
            s = s + xy_in[k, j]
        z_in[k, me_z] = s
        for j, dev in z_peers:
            z_copy(k, j, dev).start()

    def ga_at(j):
        return pl.ds(core * HALF + j * PIECE, PIECE)

    def ga_copy(k, j, dev):
        return pltpu.make_async_remote_copy(
            src_ref=total.at[k, ga_at(me_xy)], dst_ref=total.at[k, ga_at(me_xy)],
            send_sem=ga_send.at[k, j], recv_sem=ga_recv.at[k, me_xy], device_id=dev, device_id_type=MESH,
        )

    def ga_wait(k, j):
        return pltpu.make_async_remote_copy(
            src_ref=total.at[k, ga_at(j)], dst_ref=total.at[k, ga_at(j)],
            send_sem=ga_send.at[k, j], recv_sem=ga_recv.at[k, j], device_id=xy_dev(j), device_id_type=MESH,
        )

    def z_finish(k):
        others(NZZ, me_z, lambda j: z_wait(k, j).wait_recv())
        s = z_in[k, 0]
        for j in range(1, NZZ):
            s = s + z_in[k, j]
        total[k, ga_at(me_xy)] = s
        cg_copy(k, core, me_xy).start()
        for j, dev in xy_peers:
            ga_copy(k, j, dev).start()

    def cg_copy(k, which, j):
        at = pl.ds(which * HALF + j * PIECE, PIECE)
        return pltpu.make_async_remote_copy(
            src_ref=total.at[k, at], dst_ref=total.at[k, at],
            send_sem=cg_send.at[k, j], recv_sem=cg_recv.at[k, j], device_id=sibling, device_id_type=MESH,
        )

    def gather_finish(k):
        for j, _ in reversed(xy_peers):
            ga_wait(k, j).wait_recv()
            cg_copy(k, core, j).start()

    def drain(k):
        others(NSP, sp, lambda j: st_copy(k, j, sp_dev(j)).wait_send())
        others(NXY, me_xy, lambda j: xy_copy(k, j, xy_dev(j)).wait_send())
        others(NXY, me_xy, lambda j: ga_copy(k, j, xy_dev(j)).wait_send())
        others(NZZ, me_z, lambda j: z_copy(k, j, z_dev(j)).wait_send())
        c_copy(k).wait_send()
        all_sent(k)

    def all_finish(k):
        def step(j, carry):
            cg_copy(k, 1 - core, j).wait_recv()
            return carry
        lax.fori_loop(0, NXY, step, 0)

    def all_sent(k):
        def step(j, carry):
            cg_copy(k, core, j).wait_send()
            return carry
        lax.fori_loop(0, NXY, step, 0)

    sides(him, 0, 0)
    lhs = jnp.concatenate(
        [
            jnp.concatenate(
                [
                    gim[zi + 1 - dz, C : 2 * C, NY * (2 - dx) : NY * (2 - dx) + L]
                    for dz in range(3)
                    for dx in range(3)
                ],
                axis=0,
            )
            for zi in range(1, NZ + 1)
        ],
        axis=1,
    )
    acc[...] = dot_nt(lhs, jnp.concatenate([him[zi] for zi in range(NZ)], axis=1))
    pack(0, 0, acc[0:SPLIT], slopes)
    pack(0, 1, acc[SPLIT : 2 * SPLIT], jnp.zeros((8, NY), F32))
    core_start(0)
    core_finish(0)

    slope, slope_dot = st_finish(1)
    spread(4, gain * inv_std)
    spread(5, slope)
    spread(6, slope_dot)

    def before(zi, carry):
        for xb in range(NX):
            at = slice(NY * xb, NY * (xb + 1))
            gp = cols[4] * (gh[zi, :, at] - cols[5] - pre[zi, :, at] * cols[6])
            pim[zi, C : 2 * C, NY * (xb + 1) : NY * (xb + 2)] = gp.astype(BF16)
        return carry

    lax.fori_loop(1, NZ + 1, before, 0)
    halo_start(*p_halo)

    def grad_one(p):
        def block(zi, i):
            b = 4 * p + i
            dz, dx = b // 3, b % 3
            return pim[zi + 1 - dz, C : 2 * C, pl.ds(pl.multiple_of(NY * (2 - dx), NY), L)]

        lhs = jnp.concatenate(
            [
                jnp.concatenate([block(zi, i) for i in range(5)], axis=0)
                for zi in range(1, NZ + 1)
            ],
            axis=1,
        )
        inner = slice(NY, NY + L)
        rhs = jnp.concatenate([xim[zi, :, inner] for zi in range(1, NZ + 1)], axis=1)
        acc[0 : 5 * C] = dot_nt(lhs, rhs)
        face = jnp.concatenate(
            [pim[1 + (NZ - 1) * p, C : 2 * C, NY * (2 - dx) : NY * (2 - dx) + L] for dx in range(3)], axis=0
        )
        rows = pl.ds(pl.multiple_of(2 * C * p, 8), 3 * C)
        acc[rows] += dot_nt(face, xim[(NZ + 1) * p, :, inner])
        pack(1, p, acc[pl.ds(pl.multiple_of((C // 2) * p, 8), SPLIT)], jnp.zeros((8, NY), F32))

    def two_halves(h, carry):
        grad_one(h * core + (1 - h) * (1 - core))

        @pl.when(h == 0)
        def _():
            core_start(1)
        return carry

    lax.fori_loop(0, 2, two_halves, 0)
    core_finish(1)

    xy_finish(0)
    sides(pim, 1, NY)
    conv_inner(pim, w1f, gh)
    z_finish(0)
    xy_finish(1)
    halo_wait(*p_halo)

    face_planes(hp, pim)
    conv_faces(pim, w1f, gh)

    def finish(zi, carry):
        for xb in range(NX):
            v = gh[zi, :, NY * xb : NY * (xb + 1)]
            up = gim[zi, C : 2 * C, NY * (xb + 1) : NY * (xb + 2)]
            tmp[pl.ds(xb, C, stride=NX), :] = v + up.astype(F32)
        out_ref[:, pl.ds(zi - 1, 1)] = tmp[...].reshape(C, 1, NX, NY).astype(BF16)
        return carry

    lax.fori_loop(1, NZ + 1, finish, 0)
    gather_finish(0)
    z_finish(1)
    all_finish(0)
    separate(total, 0, g2_ref)
    gather_finish(1)
    drain(0)
    all_finish(1)
    drain(1)


def separate(total, k, dst, done=None):
    main, tail = [], []
    for p in range(2):
        base = p * HALF
        rest = [total[k, base + SPLIT : base + SPLIT + 32, 16 * r : 16 * (r + 1)] for r in range(7)]
        rest[6] = rest[6][0 : SPLIT - 192]
        main.append(total[k, base : base + SPLIT])
        tail.append(jnp.concatenate(rest, axis=0))
    main, tail = jnp.concatenate(main, axis=0), jnp.concatenate(tail, axis=0)
    for b in range(9):
        rows = slice(b * C, (b + 1) * C)
        m = main[rows]
        dst[3 * b] = m[:, 0:C]
        dst[3 * b + 1] = m[:, C : 2 * C]
        dst[3 * b + 2] = jnp.concatenate([m[:, 2 * C : NY], tail[rows]], axis=1)
        if done is not None and b % 3 == 2:
            done(b // 3)


def results(
    raw, total, g2_raw, out_ref, g1_ref, g2_ref, gain_ref, bias_ref, g1, gain, bias, sem
):
    def copy(i, src, dst):
        each = pltpu.make_async_copy(src, dst, sem.at[i])
        each.start()
        return each

    copies = [copy(0, raw, out_ref), copy(1, g2_raw, g2_ref)]
    row = SPLIT + 32
    bias[...] = total[0, row : row + 1, 0:C]
    gain[...] = total[0, row + 1 : row + 2, 0:C]
    copies += [copy(2, gain, gain_ref), copy(3, bias, bias_ref)]

    def send(third):
        at = pl.ds(9 * third, 9)
        copies.append(copy(4 + third, g1.at[at], g1_ref.at[at]))

    separate(total, 1, g1, send)
    for each in copies:
        each.wait()


def local(features, upstream, weight_one, weight_two, norm_gain, norm_bias):
    w1 = jnp.transpose(weight_one, (2, 3, 4, 0, 1)).reshape(27, C, C)
    w2 = jnp.transpose(weight_two, (2, 3, 4, 0, 1)).reshape(27, C, C)
    vmem = pl.BlockSpec(memory_space=pltpu.VMEM)
    dma = pltpu.SemaphoreType.DMA
    far = pl.BlockSpec(memory_space=pltpu.HBM)
    raw, total, g2_raw = pl.pallas_call(
        kernel,
        out_shape=(
            pltpu.VMEM((C, NZ, NX, NY), BF16),
            pltpu.VMEM((2, ROWS, NY), F32),
            pltpu.VMEM((27, C, C), F32),
        ),
        in_specs=[far] * 6,
        out_specs=(vmem,) * 3,
        scratch_shapes=[
            pltpu.VMEM((C, NZ, NX, NY), BF16),
            pltpu.VMEM((C, NZ, NX, NY), BF16),
            pltpu.VMEM((27, C, C), BF16),
            pltpu.VMEM((27, C, C), BF16),
            pltpu.VMEM((1, C), F32),
            pltpu.VMEM((1, C), F32),
            dma((6,)),
            pltpu.VMEM((NZ + 2, 3 * C, LP), BF16),
            pltpu.VMEM((NZ + 2, 3 * C, LP), BF16),
            pltpu.VMEM((NZ, 3 * C, L), BF16),
            pltpu.VMEM((NZ + 2, 3 * C, LP), BF16),
            pltpu.VMEM((NZ + 2, C, L), F32),
            pltpu.VMEM((NZ + 2, C, L), F32),
            pltpu.VMEM((C * NX, NY), F32),
            pltpu.VMEM((2, C, L), BF16),
            pltpu.VMEM((2, C, L), BF16),
            pltpu.VMEM((2, C, L), BF16),
            pltpu.VMEM((3 * C, 9 * C), BF16),
            pltpu.VMEM((3 * C, 9 * C), BF16),
            pltpu.VMEM((3 * C, 9 * C), BF16),
            pltpu.VMEM((2, NSP, 8, NY), F32),
            pltpu.VMEM((7, C, NY), F32),
            pltpu.VMEM((9 * C, 3 * C), F32),
            pltpu.VMEM((2, ROWS, NY), F32),
            pltpu.VMEM((2, HALF, NY), F32),
            pltpu.VMEM((2, HALF, NY), F32),
            pltpu.VMEM((2, NXY, PIECE, NY), F32),
            pltpu.VMEM((2, NZZ, PIECE, NY), F32),
            dma((3, 2)), dma((3, 2)),
            dma((2, NSP)), dma((2, NSP)),
            dma((2,)), dma((2,)),
            dma((2, NXY)), dma((2, NXY)),
            dma((2, NZZ)), dma((2, NZZ)),
            dma((2, NXY)), dma((2, NXY)),
            dma((2, NXY)), dma((2, NXY)),
        ],
        compiler_params=pltpu.CompilerParams(
            collective_id=0, has_side_effects=True, vmem_limit_bytes=56 * 1024 * 1024
        ),
    )(
        features.reshape(C, NZ, NX, NY),
        upstream.reshape(C, NZ, NX, NY),
        w1,
        w2,
        norm_gain.reshape(1, C),
        norm_bias.reshape(1, C),
    )

    out, g1, g2, gain, bias = pl.pallas_call(
        results,
        out_shape=(
            jax.ShapeDtypeStruct((C, NZ, NX, NY), BF16),
            jax.ShapeDtypeStruct((27, C, C), F32),
            jax.ShapeDtypeStruct((27, C, C), F32),
            jax.ShapeDtypeStruct((1, C), F32),
            jax.ShapeDtypeStruct((1, C), F32),
        ),
        in_specs=[vmem] * 3,
        out_specs=(far,) * 5,
        scratch_shapes=[
            pltpu.VMEM((27, C, C), F32),
            pltpu.VMEM((1, C), F32),
            pltpu.VMEM((1, C), F32),
            dma((7,)),
        ],
    )(*(pltpu.with_memory_space_constraint(v, pltpu.VMEM) for v in (raw, total, g2_raw)))

    def grad(m):
        return jnp.transpose(m.reshape(3, 3, 3, C, C), (3, 4, 0, 1, 2))

    return out.reshape(1, C, NZ, NX, NY), grad(g1), grad(g2), gain.reshape(C), bias.reshape(C)


def solution(mesh):
    cells = P("dp", None, "space", None, None)
    return jax.shard_map(
        local,
        mesh=mesh,
        in_specs=(cells, cells, P(), P(), P(), P()),
        out_specs=(cells, P(), P(), P(), P()),
        check_vma=False,
    )
```

```python
import functools

import jax
import jax.numpy as jnp
from jax import lax
from jax.experimental import pallas as pl
from jax.experimental.pallas import tpu as pltpu
from jax.sharding import PartitionSpec as P

MESH = pl.DeviceIdType.MESH
F32 = jnp.float32
BF16 = jnp.bfloat16
C = 48
NZ, NX, NY = 8, 8, 128
CELLS = 64.0 * NX * NY
EPS = 1e-5
L = NX * NY
LP = L + 2 * NY
SZ_HI, SY, SX, SZ_LO = 2, 4, 4, 4
NXY = SX * SY
NZZ = SZ_HI * SZ_LO
NSP = SZ_HI * SY
ROWS = 512
HALF = ROWS // 2
PIECE = HALF // NXY
SPLIT = 9 * C // 2


def dot(a, b):
    return lax.dot_general(a, b, (((1,), (0,)), ((), ())), preferred_element_type=F32)


def dot_nt(a, b):
    return lax.dot_general(a, b, (((1,), (1,)), ((), ())), preferred_element_type=F32)


def kernel(
    x_hbm, g_hbm, w1_hbm, w2_hbm, gain_hbm, bias_hbm,
    out_ref, total, g2_ref,
    x_ref, g_ref, w1_ref, w2_ref, gain_ref, bias_ref, load,
    xim, gim, him, pim, pre, gh, tmp, hx, hg, hp, w1c, w2f, w1f,
    st, cols, acc, part, core_in, half_sum, xy_in, z_in,
    halo_send, halo_recv, st_send, st_recv, c_send, c_recv, xy_send, xy_recv, z_send, z_recv,
    ga_send, ga_recv, cg_send, cg_recv,
):
    sp = lax.axis_index("space")
    dp = lax.axis_index("dp")
    z_hi, y = sp // SY, sp % SY
    xx_, z_lo, core = dp // (SZ_LO * 2), (dp // 2) % SZ_LO, dp % 2
    me_xy = xx_ * SY + y
    me_z = z_hi * SZ_LO + z_lo
    sibling = (sp, dp + 1 - 2 * core)

    def xy_dev(j):
        return (z_hi * SY + j % SY, (j // SY) * (SZ_LO * 2) + z_lo * 2 + core)

    def z_dev(j):
        return ((j // SZ_LO) * SY + y, xx_ * (SZ_LO * 2) + (j % SZ_LO) * 2 + core)

    ys = [(y + o) % SY for o in range(SY)]
    xs = [(xx_ + o) % SX for o in range(SX)]
    hops = (0, 1, 2, 1)
    offsets = sorted(((a, b) for a in range(SX) for b in range(SY)), key=lambda o: -hops[o[0]] - hops[o[1]])
    xy_peers = [
        (xs[a] * SY + ys[b], (z_hi * SY + ys[b], xs[a] * (SZ_LO * 2) + z_lo * 2 + core))
        for a, b in offsets[:-1]
    ]
    sp_peers = [
        (side * SY + ys[b], (side * SY + ys[b], dp))
        for side, bs in ((1 - z_hi, (2, 1, 3, 0)), (z_hi, (2, 1, 3)))
        for b in bs
    ]
    z_ids = [(me_z + o) % NZZ for o in (4, 3, 5, 2, 6, 1, 7)]
    z_peers = [(j, z_dev(j)) for j in z_ids]

    loads = [
        pltpu.make_async_copy(src, dst, load.at[i])
        for i, (src, dst) in enumerate(
            ((x_hbm, x_ref), (w1_hbm, w1_ref), (w2_hbm, w2_ref), (g_hbm, g_ref), (gain_hbm, gain_ref), (bias_hbm, bias_ref))
        )
    ]
    for each in loads:
        each.start()

    barrier = pltpu.get_barrier_semaphore()

    def greet(dev):
        pl.semaphore_signal(barrier, inc=1, device_id=dev, device_id_type=MESH)

    for _, dev in sp_peers + z_peers + xy_peers:
        greet(dev)
    greet(sibling)

    lane = lax.broadcasted_iota(jnp.int32, (C, NY), 1)
    eye = lax.broadcasted_iota(jnp.int32, (C, NY), 0) == lane
    first, last = lane == 0, lane == NY - 1

    def column(row):
        return jnp.sum(jnp.where(eye, jnp.broadcast_to(row, (C, NY)), 0.0), axis=1, keepdims=True)

    def as_row(col):
        return jnp.sum(jnp.where(eye, jnp.broadcast_to(col, (C, NY)), 0.0), axis=0, keepdims=True)

    def put_sides(im, zi, at, v):
        im[zi, 0:C, at] = jnp.where(first, 0.0, pltpu.roll(v, 1, 1)).astype(BF16)
        im[zi, 2 * C : 3 * C, at] = jnp.where(last, 0.0, pltpu.roll(v, NY - 1, 1)).astype(BF16)

    def put(im, zi, lo, v):
        at = pl.ds(lo, NY)
        im[zi, C : 2 * C, at] = v.astype(BF16)
        put_sides(im, zi, at, v)

    def sides(im, begin, lo):
        def step(zi, carry):
            for xb in range(NX):
                at = pl.ds(lo + NY * xb, NY)
                put_sides(im, zi, at, im[zi, C : 2 * C, at].astype(F32))
            return carry
        lax.fori_loop(begin, begin + NZ, step, 0)

    def unpack(raw, im, zi):
        tmp[...] = raw.astype(F32).reshape(C * NX, NY)
        for xb in range(NX):
            put(im, zi, NY * (xb + 1), tmp[pl.ds(xb, C, stride=NX), :])

    edge = jnp.zeros((3 * C, NY), BF16)

    def zero_edges(zi, carry):
        for im in (xim, gim, pim):
            im[zi, :, 0:NY] = edge
            im[zi, :, LP - NY : LP] = edge
        return carry

    lax.fori_loop(0, NZ + 2, zero_edges, 0)
    pim[0, C : 2 * C, :] = jnp.zeros((C, LP), BF16)
    pim[NZ + 1, C : 2 * C, :] = jnp.zeros((C, LP), BF16)

    def unpack_own(src, im):
        def step(zi, carry):
            unpack(src[:, pl.ds(zi, 1)].reshape(C, NX, NY), im, zi + 1)
            return carry
        lax.fori_loop(0, NZ, step, 0)

    loads[0].wait()
    unpack_own(x_ref, xim)

    loads[1].wait()
    loads[2].wait()
    for dz in range(3):
        rows = slice(dz * C, (dz + 1) * C)
        blocks = [w1_ref[dz * 9 + t].astype(F32).T for t in range(9)]
        w1c[rows, :] = jnp.concatenate(blocks, axis=0).T.astype(BF16)
        for w_ref, dst in ((w2_ref, w2f), (w1_ref, w1f)):
            blocks = [w_ref[26 - (dz * 9 + t)].astype(F32) for t in range(9)]
            dst[rows, :] = jnp.concatenate(blocks, axis=0).T.astype(BF16)

    has_up, has_down = sp < NSP - 1, sp > 0

    def halo_copy(src, dst, k, slot, dev):
        return pltpu.make_async_remote_copy(
            src_ref=src, dst_ref=dst.at[slot], send_sem=halo_send.at[k, slot],
            recv_sem=halo_recv.at[k, slot], device_id=dev, device_id_type=MESH,
        )

    def halo_start(low, high, dst, k):
        @pl.when(has_up)
        def _():
            halo_copy(high, dst, k, 0, (sp + 1, dp)).start()

        @pl.when(has_down)
        def _():
            halo_copy(low, dst, k, 1, (sp - 1, dp)).start()

    def halo_wait(low, high, dst, k):
        @pl.when(has_up)
        def _():
            halo_copy(high, dst, k, 0, (sp + 1, dp)).wait_send()
            halo_copy(high, dst, k, 1, (sp + 1, dp)).wait_recv()

        @pl.when(has_down)
        def _():
            halo_copy(low, dst, k, 1, (sp - 1, dp)).wait_send()
            halo_copy(low, dst, k, 0, (sp - 1, dp)).wait_recv()

    def halo_of(im, dst, k):
        at = (slice(C, 2 * C), slice(NY, NY + L))
        return im.at[(1,) + at], im.at[(NZ,) + at], dst, k

    x_halo = halo_of(xim, hx, 0)
    g_halo = halo_of(gim, hg, 1)
    p_halo = halo_of(pim, hp, 2)

    def window(im, zi):
        return jnp.concatenate([im[zi, :, NY * d : NY * d + L] for d in range(3)], axis=0)

    def conv_inner(im, w, dst):
        dst[0] = jnp.zeros((C, L), F32)
        dst[1] = jnp.zeros((C, L), F32)

        def step(zi, carry):
            p = dot(w[...], window(im, zi))
            dst[zi + 1] = p[0:C]
            dst[zi] += p[C : 2 * C]
            dst[zi - 1] += p[2 * C : 3 * C]
            return carry

        lax.fori_loop(1, NZ + 1, step, 0)

    def conv_faces(im, w, dst):
        dst[1] += dot(w[0:C], window(im, 0))
        dst[NZ] += dot(w[2 * C : 3 * C], window(im, NZ + 1))

    def face_planes(dst, im):
        for slot, zi, live in ((0, 0, has_down), (1, NZ + 1, has_up)):
            for xb in range(NX):
                v = dst[slot, :, NY * xb : NY * (xb + 1)].astype(F32)
                put(im, zi, NY * (xb + 1), jnp.where(live, v, 0.0))

    def st_copy(k, j, dev):
        return pltpu.make_async_remote_copy(
            src_ref=st.at[k, sp], dst_ref=st.at[k, sp], send_sem=st_send.at[k],
            recv_sem=st_recv.at[k], device_id=dev, device_id_type=MESH,
        )

    def bulk(ref, send, recv):
        return pltpu.make_async_remote_copy(
            src_ref=ref, dst_ref=ref, send_sem=send, recv_sem=recv, device_id=sibling, device_id_type=MESH,
        )

    def st_all(k):
        return bulk(st.at[k, 0 : NSP - 1], st_send.at[k], st_recv.at[k])

    def st_start(k, one, two):
        row_one = as_row(jnp.sum(one, axis=1, keepdims=True))
        row_two = as_row(jnp.sum(two, axis=1, keepdims=True))
        lead = lax.broadcasted_iota(jnp.int32, (8, NY), 0)
        mine = jnp.where(lead == 0, row_one, 0.0) + jnp.where(lead == 1, row_two, 0.0)
        st[k, sp] = mine
        for j, dev in sp_peers:
            st_copy(k, j, dev).start()
        return mine

    def st_finish(k):
        st_all(k).wait_recv()
        s = st[k, 0]
        for j in range(1, NSP):
            s = s + st[k, j]
        return column(s[0:1] / CELLS), column(s[1:2] / CELLS)

    conv_inner(xim, w1c, pre)
    pl.semaphore_wait(barrier, 1 + (NSP - 1) + (NXY - 1) + (NZZ - 1))

    halo_start(*x_halo)
    loads[3].wait()
    unpack_own(g_ref, gim)
    conv_inner(gim, w2f, gh)
    halo_start(*g_halo)

    zero = jnp.zeros((C, NY), F32)

    def moments(zi, carry):
        one, two = carry
        for xb in range(NX):
            v = pre[zi, :, NY * xb : NY * (xb + 1)]
            one, two = one + v, two + v * v
        return one, two

    sums = lax.fori_loop(2, NZ, moments, (zero, zero))
    halo_wait(*x_halo)
    face_planes(hx, xim)
    conv_faces(xim, w1c, pre)
    st_start(0, *moments(NZ, moments(1, sums)))

    halo_wait(*g_halo)
    face_planes(hg, gim)
    conv_faces(gim, w2f, gh)

    loads[4].wait()
    loads[5].wait()
    pad = jnp.zeros((1, NY - C), F32)
    def spread(i, col):
        cols[i] = jnp.broadcast_to(col, (C, NY))

    gain = column(jnp.concatenate([gain_ref[...], pad], axis=1))
    spread(2, gain)
    spread(3, column(jnp.concatenate([bias_ref[...], pad], axis=1)))
    mean, square = st_finish(0)
    inv_std = lax.rsqrt(square - mean * mean + EPS)
    spread(0, mean)
    spread(1, inv_std)

    def activate(zi, carry):
        one, two = carry
        for xb in range(NX):
            at = slice(NY * xb, NY * (xb + 1))
            hat = (pre[zi, :, at] - cols[0]) * cols[1]
            normed = hat * cols[2] + cols[3]
            sig = jax.nn.sigmoid(normed)
            act = normed * sig
            him[zi - 1, C : 2 * C, at] = act.astype(BF16)
            gn = gh[zi, :, at] * (sig + act * (1.0 - sig))
            gh[zi, :, at] = gn
            pre[zi, :, at] = hat
            one, two = one + gn, two + gn * hat
        return one, two

    slopes = st_start(1, *lax.fori_loop(1, NZ + 1, activate, (zero, zero)))

    def c_copy(k):
        return pltpu.make_async_remote_copy(
            src_ref=part.at[k, pl.ds((1 - core) * HALF, HALF)], dst_ref=core_in.at[k],
            send_sem=c_send.at[k], recv_sem=c_recv.at[k], device_id=sibling, device_id_type=MESH,
        )

    def pack(k, p, v, tail):
        base = p * HALF
        part[k, pl.ds(base, SPLIT)] = v[:, 0:NY]
        rest = jnp.concatenate([v[:, NY : NY + 16], jnp.zeros((256 - SPLIT, 16), F32)], axis=0)
        pieces = [rest[32 * r : 32 * (r + 1)] for r in range(8)]
        part[k, pl.ds(base + SPLIT, 32)] = jnp.concatenate(pieces, axis=1)
        part[k, pl.ds(base + SPLIT + 32, 8)] = tail

    def core_start(k):
        c_copy(k).start()

    def xy_copy(k, j, dev):
        return pltpu.make_async_remote_copy(
            src_ref=half_sum.at[k, pl.ds(j * PIECE, PIECE)], dst_ref=xy_in.at[k, me_xy],
            send_sem=xy_send.at[k], recv_sem=xy_recv.at[k], device_id=dev, device_id_type=MESH,
        )

    def xy_all(k):
        return bulk(xy_in.at[k, 0 : NXY - 1], xy_send.at[k], xy_recv.at[k])

    def core_finish(k):
        c_copy(k).wait_recv()
        half_sum[k] = part[k, pl.ds(core * HALF, HALF)] + core_in[k]
        for j, dev in xy_peers:
            xy_copy(k, j, dev).start()

    def z_copy(k, j, dev):
        return pltpu.make_async_remote_copy(
            src_ref=z_in.at[k, me_z], dst_ref=z_in.at[k, me_z],
            send_sem=z_send.at[k], recv_sem=z_recv.at[k], device_id=dev, device_id_type=MESH,
        )

    def z_all(k):
        return bulk(z_in.at[k, 0 : NZZ - 1], z_send.at[k], z_recv.at[k])

    def xy_finish(k):
        xy_all(k).wait_recv()
        xy_in[k, me_xy] = half_sum[k, pl.ds(me_xy * PIECE, PIECE)]
        s = xy_in[k, 0]
        for j in range(1, NXY):
            s = s + xy_in[k, j]
        z_in[k, me_z] = s
        for j, dev in z_peers:
            z_copy(k, j, dev).start()

    def ga_at(j):
        return pl.ds(core * HALF + j * PIECE, PIECE)

    def ga_copy(k, j, dev):
        return pltpu.make_async_remote_copy(
            src_ref=total.at[k, ga_at(me_xy)], dst_ref=total.at[k, ga_at(me_xy)],
            send_sem=ga_send.at[k], recv_sem=ga_recv.at[k, me_xy], device_id=dev, device_id_type=MESH,
        )

    def ga_wait(k, j):
        return pltpu.make_async_remote_copy(
            src_ref=total.at[k, ga_at(j)], dst_ref=total.at[k, ga_at(j)],
            send_sem=ga_send.at[k], recv_sem=ga_recv.at[k, j], device_id=xy_dev(j), device_id_type=MESH,
        )

    def z_finish(k):
        z_all(k).wait_recv()
        s = z_in[k, 0]
        for j in range(1, NZZ):
            s = s + z_in[k, j]
        total[k, ga_at(me_xy)] = s
        cg_copy(k, core, me_xy).start()
        for j, dev in xy_peers:
            ga_copy(k, j, dev).start()

    def cg_copy(k, which, j):
        at = pl.ds(which * HALF + j * PIECE, PIECE)
        return pltpu.make_async_remote_copy(
            src_ref=total.at[k, at], dst_ref=total.at[k, at],
            send_sem=cg_send.at[k], recv_sem=cg_recv.at[k], device_id=sibling, device_id_type=MESH,
        )

    def gather_finish(k):
        for j, _ in reversed(xy_peers):
            ga_wait(k, j).wait_recv()
            cg_copy(k, core, j).start()

    def cg_half(k, which):
        return bulk(total.at[k, pl.ds(which * HALF, HALF)], cg_send.at[k], cg_recv.at[k])

    def ga_sent(k):
        bulk(total.at[k, 0 : HALF - PIECE], ga_send.at[k], ga_recv.at[k, 0]).wait_send()

    def drain(k):
        st_all(k).wait_send()
        xy_all(k).wait_send()
        z_all(k).wait_send()
        c_copy(k).wait_send()

    def all_finish(k):
        cg_half(k, 1 - core).wait_recv()

    sides(him, 0, 0)
    lhs = jnp.concatenate(
        [
            jnp.concatenate(
                [
                    gim[zi + 1 - dz, C : 2 * C, NY * (2 - dx) : NY * (2 - dx) + L]
                    for dz in range(3)
                    for dx in range(3)
                ],
                axis=0,
            )
            for zi in range(1, NZ + 1)
        ],
        axis=1,
    )
    acc[...] = dot_nt(lhs, jnp.concatenate([him[zi] for zi in range(NZ)], axis=1))
    pack(0, 0, acc[0:SPLIT], slopes)
    pack(0, 1, acc[SPLIT : 2 * SPLIT], jnp.zeros((8, NY), F32))
    core_start(0)
    core_finish(0)

    slope, slope_dot = st_finish(1)
    spread(4, gain * inv_std)
    spread(5, slope)
    spread(6, slope_dot)

    def before(zi, carry):
        for xb in range(NX):
            at = slice(NY * xb, NY * (xb + 1))
            gp = cols[4] * (gh[zi, :, at] - cols[5] - pre[zi, :, at] * cols[6])
            pim[zi, C : 2 * C, NY * (xb + 1) : NY * (xb + 2)] = gp.astype(BF16)
        return carry

    lax.fori_loop(1, NZ + 1, before, 0)
    halo_start(*p_halo)

    def grad_one(p):
        def block(zi, i):
            b = 4 * p + i
            dz, dx = b // 3, b % 3
            return pim[zi + 1 - dz, C : 2 * C, pl.ds(pl.multiple_of(NY * (2 - dx), NY), L)]

        lhs = jnp.concatenate(
            [
                jnp.concatenate([block(zi, i) for i in range(5)], axis=0)
                for zi in range(1, NZ + 1)
            ],
            axis=1,
        )
        inner = slice(NY, NY + L)
        rhs = jnp.concatenate([xim[zi, :, inner] for zi in range(1, NZ + 1)], axis=1)
        acc[0 : 5 * C] = dot_nt(lhs, rhs)
        face = jnp.concatenate(
            [pim[1 + (NZ - 1) * p, C : 2 * C, NY * (2 - dx) : NY * (2 - dx) + L] for dx in range(3)], axis=0
        )
        rows = pl.ds(pl.multiple_of(2 * C * p, 8), 3 * C)
        acc[rows] += dot_nt(face, xim[(NZ + 1) * p, :, inner])
        pack(1, p, acc[pl.ds(pl.multiple_of((C // 2) * p, 8), SPLIT)], jnp.zeros((8, NY), F32))

    def two_halves(h, carry):
        grad_one(h * core + (1 - h) * (1 - core))

        @pl.when(h == 0)
        def _():
            core_start(1)
        return carry

    lax.fori_loop(0, 2, two_halves, 0)
    core_finish(1)

    sides(pim, 1, NY)
    xy_finish(0)
    conv_inner(pim, w1f, gh)
    xy_finish(1)
    z_finish(0)
    halo_wait(*p_halo)

    face_planes(hp, pim)
    conv_faces(pim, w1f, gh)

    def finish(zi, carry):
        for xb in range(NX):
            v = gh[zi, :, NY * xb : NY * (xb + 1)]
            up = gim[zi, C : 2 * C, NY * (xb + 1) : NY * (xb + 2)]
            tmp[pl.ds(xb, C, stride=NX), :] = v + up.astype(F32)
        out_ref[:, pl.ds(zi - 1, 1)] = tmp[...].reshape(C, 1, NX, NY).astype(BF16)
        return carry

    lax.fori_loop(1, NZ + 1, finish, 0)
    z_finish(1)
    gather_finish(0)
    all_finish(0)
    separate(total, 0, g2_ref)
    drain(0)
    drain(1)
    ga_sent(0)
    cg_half(0, core).wait_send()
    gather_finish(1)
    ga_sent(1)
    all_finish(1)
    cg_half(1, core).wait_send()


def separate(total, k, dst, done=None):
    main, tail = [], []
    for p in range(2):
        base = p * HALF
        rest = [total[k, base + SPLIT : base + SPLIT + 32, 16 * r : 16 * (r + 1)] for r in range(7)]
        rest[6] = rest[6][0 : SPLIT - 192]
        main.append(total[k, base : base + SPLIT])
        tail.append(jnp.concatenate(rest, axis=0))
    main, tail = jnp.concatenate(main, axis=0), jnp.concatenate(tail, axis=0)
    for b in range(9):
        rows = slice(b * C, (b + 1) * C)
        m = main[rows]
        dst[3 * b] = m[:, 0:C]
        dst[3 * b + 1] = m[:, C : 2 * C]
        dst[3 * b + 2] = jnp.concatenate([m[:, 2 * C : NY], tail[rows]], axis=1)
        if done is not None and b % 3 == 2:
            done(b // 3)


def results(
    raw, total, g2_raw, out_ref, g1_ref, g2_ref, gain_ref, bias_ref, g1, gain, bias, sem
):
    def copy(i, src, dst):
        each = pltpu.make_async_copy(src, dst, sem.at[i])
        each.start()
        return each

    copies = [copy(0, raw, out_ref), copy(1, g2_raw, g2_ref)]
    row = SPLIT + 32
    bias[...] = total[0, row : row + 1, 0:C]
    gain[...] = total[0, row + 1 : row + 2, 0:C]
    copies += [copy(2, gain, gain_ref), copy(3, bias, bias_ref)]

    def send(third):
        at = pl.ds(9 * third, 9)
        copies.append(copy(4 + third, g1.at[at], g1_ref.at[at]))

    separate(total, 1, g1, send)
    for each in copies:
        each.wait()


def local(features, upstream, weight_one, weight_two, norm_gain, norm_bias):
    w1 = jnp.transpose(weight_one, (2, 3, 4, 0, 1)).reshape(27, C, C)
    w2 = jnp.transpose(weight_two, (2, 3, 4, 0, 1)).reshape(27, C, C)
    vmem = pl.BlockSpec(memory_space=pltpu.VMEM)
    dma = pltpu.SemaphoreType.DMA
    far = pl.BlockSpec(memory_space=pltpu.HBM)
    raw, total, g2_raw = pl.pallas_call(
        kernel,
        out_shape=(
            pltpu.VMEM((C, NZ, NX, NY), BF16),
            pltpu.VMEM((2, ROWS, NY), F32),
            pltpu.VMEM((27, C, C), F32),
        ),
        in_specs=[far] * 6,
        out_specs=(vmem,) * 3,
        scratch_shapes=[
            pltpu.VMEM((C, NZ, NX, NY), BF16),
            pltpu.VMEM((C, NZ, NX, NY), BF16),
            pltpu.VMEM((27, C, C), BF16),
            pltpu.VMEM((27, C, C), BF16),
            pltpu.VMEM((1, C), F32),
            pltpu.VMEM((1, C), F32),
            dma((6,)),
            pltpu.VMEM((NZ + 2, 3 * C, LP), BF16),
            pltpu.VMEM((NZ + 2, 3 * C, LP), BF16),
            pltpu.VMEM((NZ, 3 * C, L), BF16),
            pltpu.VMEM((NZ + 2, 3 * C, LP), BF16),
            pltpu.VMEM((NZ + 2, C, L), F32),
            pltpu.VMEM((NZ + 2, C, L), F32),
            pltpu.VMEM((C * NX, NY), F32),
            pltpu.VMEM((2, C, L), BF16),
            pltpu.VMEM((2, C, L), BF16),
            pltpu.VMEM((2, C, L), BF16),
            pltpu.VMEM((3 * C, 9 * C), BF16),
            pltpu.VMEM((3 * C, 9 * C), BF16),
            pltpu.VMEM((3 * C, 9 * C), BF16),
            pltpu.VMEM((2, NSP, 8, NY), F32),
            pltpu.VMEM((7, C, NY), F32),
            pltpu.VMEM((9 * C, 3 * C), F32),
            pltpu.VMEM((2, ROWS, NY), F32),
            pltpu.VMEM((2, HALF, NY), F32),
            pltpu.VMEM((2, HALF, NY), F32),
            pltpu.VMEM((2, NXY, PIECE, NY), F32),
            pltpu.VMEM((2, NZZ, PIECE, NY), F32),
            dma((3, 2)), dma((3, 2)),
            dma((2,)), dma((2,)),
            dma((2,)), dma((2,)),
            dma((2,)), dma((2,)),
            dma((2,)), dma((2,)),
            dma((2,)), dma((2, NXY)),
            dma((2,)), dma((2,)),
        ],
        compiler_params=pltpu.CompilerParams(
            collective_id=0, has_side_effects=True, vmem_limit_bytes=56 * 1024 * 1024
        ),
    )(
        features.reshape(C, NZ, NX, NY),
        upstream.reshape(C, NZ, NX, NY),
        w1,
        w2,
        norm_gain.reshape(1, C),
        norm_bias.reshape(1, C),
    )

    out, g1, g2, gain, bias = pl.pallas_call(
        results,
        out_shape=(
            jax.ShapeDtypeStruct((C, NZ, NX, NY), BF16),
            jax.ShapeDtypeStruct((27, C, C), F32),
            jax.ShapeDtypeStruct((27, C, C), F32),
            jax.ShapeDtypeStruct((1, C), F32),
            jax.ShapeDtypeStruct((1, C), F32),
        ),
        in_specs=[vmem] * 3,
        out_specs=(far,) * 5,
        scratch_shapes=[
            pltpu.VMEM((27, C, C), F32),
            pltpu.VMEM((1, C), F32),
            pltpu.VMEM((1, C), F32),
            dma((7,)),
        ],
    )(*(pltpu.with_memory_space_constraint(v, pltpu.VMEM) for v in (raw, total, g2_raw)))

    def grad(m):
        return jnp.transpose(m.reshape(3, 3, 3, C, C), (3, 4, 0, 1, 2))

    return out.reshape(1, C, NZ, NX, NY), grad(g1), grad(g2), gain.reshape(C), bias.reshape(C)


def solution(mesh):
    cells = P("dp", None, "space", None, None)
    return jax.shard_map(
        local,
        mesh=mesh,
        in_specs=(cells, cells, P(), P(), P(), P()),
        out_specs=(cells, P(), P(), P(), P()),
        check_vma=False,
    )
```

```python
import functools

import jax
import jax.numpy as jnp
from jax import lax
from jax.experimental import pallas as pl
from jax.experimental.pallas import tpu as pltpu
from jax.sharding import PartitionSpec as P

MESH = pl.DeviceIdType.MESH
F32 = jnp.float32
BF16 = jnp.bfloat16
C = 48
NZ, NX, NY = 8, 8, 128
CELLS = 64.0 * NX * NY
EPS = 1e-5
L = NX * NY
LP = L + 2 * NY
SZ_HI, SY, SX, SZ_LO = 2, 4, 4, 4
NXY = SX * SY
NZZ = SZ_HI * SZ_LO
NSP = SZ_HI * SY
ROWS = 512
HALF = ROWS // 2
PIECE = HALF // NXY
SPLIT = 9 * C // 2


def dot(a, b):
    return lax.dot_general(a, b, (((1,), (0,)), ((), ())), preferred_element_type=F32)


def dot_nt(a, b):
    return lax.dot_general(a, b, (((1,), (1,)), ((), ())), preferred_element_type=F32)


def kernel(
    x_hbm, g_hbm, w1_hbm, w2_hbm, gain_hbm, bias_hbm,
    out_ref, total, g2_ref,
    x_ref, g_ref, w1_ref, w2_ref, gain_ref, bias_ref, load,
    xim, gim, him, pim, pre, gh, tmp, hx, hg, hp, w1c, w2f, w1f,
    st, cols, acc, part, core_in, half_sum, xy_in, z_in,
    halo_send, halo_recv, st_send, st_recv, c_send, c_recv, xy_send, xy_recv, z_send, z_recv,
    ga_send, ga_recv, cg_send, cg_recv,
):
    sp = lax.axis_index("space")
    dp = lax.axis_index("dp")
    z_hi, y = sp // SY, sp % SY
    xx_, z_lo, core = dp // (SZ_LO * 2), (dp // 2) % SZ_LO, dp % 2
    me_xy = xx_ * SY + y
    me_z = z_hi * SZ_LO + z_lo
    sibling = (sp, dp + 1 - 2 * core)

    def xy_dev(j):
        return (z_hi * SY + j % SY, (j // SY) * (SZ_LO * 2) + z_lo * 2 + core)

    def z_dev(j):
        return ((j // SZ_LO) * SY + y, xx_ * (SZ_LO * 2) + (j % SZ_LO) * 2 + core)

    ys = [(y + o) % SY for o in range(SY)]
    xs = [(xx_ + o) % SX for o in range(SX)]
    hops = (0, 1, 2, 1)
    offsets = sorted(((a, b) for a in range(SX) for b in range(SY)), key=lambda o: -hops[o[0]] - hops[o[1]])
    xy_peers = [
        (xs[a] * SY + ys[b], (z_hi * SY + ys[b], xs[a] * (SZ_LO * 2) + z_lo * 2 + core))
        for a, b in offsets[:-1]
    ]
    sp_peers = [
        (side * SY + ys[b], (side * SY + ys[b], dp))
        for side, bs in ((1 - z_hi, (2, 1, 3, 0)), (z_hi, (2, 1, 3)))
        for b in bs
    ]
    z_ids = [(me_z + o) % NZZ for o in (4, 3, 5, 2, 6, 1, 7)]
    z_peers = [(j, z_dev(j)) for j in z_ids]

    barrier = pltpu.get_barrier_semaphore()

    def greet(dev):
        pl.semaphore_signal(barrier, inc=1, device_id=dev, device_id_type=MESH)

    for _, dev in sp_peers:
        greet(dev)

    loads = [
        pltpu.make_async_copy(src, dst, load.at[i])
        for i, (src, dst) in enumerate(
            ((x_hbm, x_ref), (w1_hbm, w1_ref), (w2_hbm, w2_ref), (g_hbm, g_ref), (gain_hbm, gain_ref), (bias_hbm, bias_ref))
        )
    ]
    for each in loads:
        each.start()

    for _, dev in z_peers + xy_peers:
        greet(dev)
    greet(sibling)

    lane = lax.broadcasted_iota(jnp.int32, (C, NY), 1)
    eye = lax.broadcasted_iota(jnp.int32, (C, NY), 0) == lane
    first, last = lane == 0, lane == NY - 1

    def column(row):
        return jnp.sum(jnp.where(eye, jnp.broadcast_to(row, (C, NY)), 0.0), axis=1, keepdims=True)

    def as_row(col):
        return jnp.sum(jnp.where(eye, jnp.broadcast_to(col, (C, NY)), 0.0), axis=0, keepdims=True)

    def put_sides(im, zi, at, v):
        im[zi, 0:C, at] = jnp.where(first, 0.0, pltpu.roll(v, 1, 1)).astype(BF16)
        im[zi, 2 * C : 3 * C, at] = jnp.where(last, 0.0, pltpu.roll(v, NY - 1, 1)).astype(BF16)

    def put(im, zi, lo, v):
        at = pl.ds(lo, NY)
        im[zi, C : 2 * C, at] = v.astype(BF16)
        put_sides(im, zi, at, v)

    def sides(im, begin, lo):
        def step(zi, carry):
            for xb in range(NX):
                at = pl.ds(lo + NY * xb, NY)
                put_sides(im, zi, at, im[zi, C : 2 * C, at].astype(F32))
            return carry
        lax.fori_loop(begin, begin + NZ, step, 0)

    def unpack(raw, im, zi):
        tmp[...] = raw.astype(F32).reshape(C * NX, NY)
        for xb in range(NX):
            put(im, zi, NY * (xb + 1), tmp[pl.ds(xb, C, stride=NX), :])

    edge = jnp.zeros((3 * C, NY), BF16)

    def zero_edges(zi, carry):
        for im in (xim, gim, pim):
            im[zi, :, 0:NY] = edge
            im[zi, :, LP - NY : LP] = edge
        return carry

    lax.fori_loop(0, NZ + 2, zero_edges, 0)
    pim[0, C : 2 * C, :] = jnp.zeros((C, LP), BF16)
    pim[NZ + 1, C : 2 * C, :] = jnp.zeros((C, LP), BF16)

    def unpack_own(src, im):
        def step(zi, carry):
            unpack(src[:, pl.ds(zi, 1)].reshape(C, NX, NY), im, zi + 1)
            return carry
        lax.fori_loop(0, NZ, step, 0)

    loads[0].wait()
    unpack_own(x_ref, xim)

    loads[1].wait()
    loads[2].wait()
    for dz in range(3):
        rows = slice(dz * C, (dz + 1) * C)
        blocks = [w1_ref[dz * 9 + t].astype(F32).T for t in range(9)]
        w1c[rows, :] = jnp.concatenate(blocks, axis=0).T.astype(BF16)
        for w_ref, dst in ((w2_ref, w2f), (w1_ref, w1f)):
            blocks = [w_ref[26 - (dz * 9 + t)].astype(F32) for t in range(9)]
            dst[rows, :] = jnp.concatenate(blocks, axis=0).T.astype(BF16)

    has_up, has_down = sp < NSP - 1, sp > 0

    def halo_copy(src, dst, k, slot, dev):
        return pltpu.make_async_remote_copy(
            src_ref=src, dst_ref=dst.at[slot], send_sem=halo_send.at[k, slot],
            recv_sem=halo_recv.at[k, slot], device_id=dev, device_id_type=MESH,
        )

    def halo_start(low, high, dst, k):
        @pl.when(has_up)
        def _():
            halo_copy(high, dst, k, 0, (sp + 1, dp)).start()

        @pl.when(has_down)
        def _():
            halo_copy(low, dst, k, 1, (sp - 1, dp)).start()

    def halo_wait(low, high, dst, k):
        @pl.when(has_up)
        def _():
            halo_copy(high, dst, k, 0, (sp + 1, dp)).wait_send()
            halo_copy(high, dst, k, 1, (sp + 1, dp)).wait_recv()

        @pl.when(has_down)
        def _():
            halo_copy(low, dst, k, 1, (sp - 1, dp)).wait_send()
            halo_copy(low, dst, k, 0, (sp - 1, dp)).wait_recv()

    def halo_of(im, dst, k):
        at = (slice(C, 2 * C), slice(NY, NY + L))
        return im.at[(1,) + at], im.at[(NZ,) + at], dst, k

    x_halo = halo_of(xim, hx, 0)
    g_halo = halo_of(gim, hg, 1)
    p_halo = halo_of(pim, hp, 2)

    def window(im, zi):
        return jnp.concatenate([im[zi, :, NY * d : NY * d + L] for d in range(3)], axis=0)

    def conv_inner(im, w, dst):
        dst[0] = jnp.zeros((C, L), F32)
        dst[1] = jnp.zeros((C, L), F32)

        def step(zi, carry):
            p = dot(w[...], window(im, zi))
            dst[zi + 1] = p[0:C]
            dst[zi] += p[C : 2 * C]
            dst[zi - 1] += p[2 * C : 3 * C]
            return carry

        lax.fori_loop(1, NZ + 1, step, 0)

    def conv_faces(im, w, dst):
        dst[1] += dot(w[0:C], window(im, 0))
        dst[NZ] += dot(w[2 * C : 3 * C], window(im, NZ + 1))

    def face_planes(dst, im):
        for slot, zi, live in ((0, 0, has_down), (1, NZ + 1, has_up)):
            for xb in range(NX):
                v = dst[slot, :, NY * xb : NY * (xb + 1)].astype(F32)
                put(im, zi, NY * (xb + 1), jnp.where(live, v, 0.0))

    def st_copy(k, j, dev):
        return pltpu.make_async_remote_copy(
            src_ref=st.at[k, sp], dst_ref=st.at[k, sp], send_sem=st_send.at[k],
            recv_sem=st_recv.at[k], device_id=dev, device_id_type=MESH,
        )

    def bulk(ref, send, recv):
        return pltpu.make_async_remote_copy(
            src_ref=ref, dst_ref=ref, send_sem=send, recv_sem=recv, device_id=sibling, device_id_type=MESH,
        )

    def st_all(k):
        return bulk(st.at[k, 0 : NSP - 1], st_send.at[k], st_recv.at[k])

    def st_start(k, one, two):
        row_one = as_row(jnp.sum(one, axis=1, keepdims=True))
        row_two = as_row(jnp.sum(two, axis=1, keepdims=True))
        lead = lax.broadcasted_iota(jnp.int32, (8, NY), 0)
        mine = jnp.where(lead == 0, row_one, 0.0) + jnp.where(lead == 1, row_two, 0.0)
        st[k, sp] = mine
        for j, dev in sp_peers:
            st_copy(k, j, dev).start()
        return mine

    def st_finish(k):
        st_all(k).wait_recv()
        s = st[k, 0]
        for j in range(1, NSP):
            s = s + st[k, j]
        return column(s[0:1] / CELLS), column(s[1:2] / CELLS)

    conv_inner(xim, w1c, pre)
    pl.semaphore_wait(barrier, 1 + (NSP - 1) + (NXY - 1) + (NZZ - 1))

    halo_start(*x_halo)
    loads[3].wait()
    unpack_own(g_ref, gim)
    conv_inner(gim, w2f, gh)
    halo_start(*g_halo)

    zero = jnp.zeros((C, NY), F32)

    def moments(zi, carry):
        one, two = carry
        for xb in range(NX):
            v = pre[zi, :, NY * xb : NY * (xb + 1)]
            one, two = one + v, two + v * v
        return one, two

    sums = lax.fori_loop(2, NZ, moments, (zero, zero))
    halo_wait(*x_halo)
    face_planes(hx, xim)
    conv_faces(xim, w1c, pre)
    st_start(0, *moments(NZ, moments(1, sums)))

    halo_wait(*g_halo)
    face_planes(hg, gim)
    conv_faces(gim, w2f, gh)

    loads[4].wait()
    loads[5].wait()
    pad = jnp.zeros((1, NY - C), F32)
    def spread(i, col):
        cols[i] = jnp.broadcast_to(col, (C, NY))

    gain = column(jnp.concatenate([gain_ref[...], pad], axis=1))
    spread(2, gain)
    spread(3, column(jnp.concatenate([bias_ref[...], pad], axis=1)))
    mean, square = st_finish(0)
    inv_std = lax.rsqrt(square - mean * mean + EPS)
    spread(0, mean)
    spread(1, inv_std)

    def activate(zi, carry):
        one, two = carry
        for xb in range(NX):
            at = slice(NY * xb, NY * (xb + 1))
            hat = (pre[zi, :, at] - cols[0]) * cols[1]
            normed = hat * cols[2] + cols[3]
            sig = jax.nn.sigmoid(normed)
            act = normed * sig
            him[zi - 1, C : 2 * C, at] = act.astype(BF16)
            gn = gh[zi, :, at] * (sig + act * (1.0 - sig))
            gh[zi, :, at] = gn
            pre[zi, :, at] = hat
            one, two = one + gn, two + gn * hat
        return one, two

    slopes = st_start(1, *lax.fori_loop(1, NZ + 1, activate, (zero, zero)))

    def c_copy(k):
        return pltpu.make_async_remote_copy(
            src_ref=part.at[k, pl.ds((1 - core) * HALF, HALF)], dst_ref=core_in.at[k],
            send_sem=c_send.at[k], recv_sem=c_recv.at[k], device_id=sibling, device_id_type=MESH,
        )

    def pack(k, p, v, tail):
        base = p * HALF
        part[k, pl.ds(base, SPLIT)] = v[:, 0:NY]
        rest = jnp.concatenate([v[:, NY : NY + 16], jnp.zeros((256 - SPLIT, 16), F32)], axis=0)
        pieces = [rest[32 * r : 32 * (r + 1)] for r in range(8)]
        part[k, pl.ds(base + SPLIT, 32)] = jnp.concatenate(pieces, axis=1)
        part[k, pl.ds(base + SPLIT + 32, 8)] = tail

    def core_start(k):
        c_copy(k).start()

    def xy_copy(k, j, dev):
        return pltpu.make_async_remote_copy(
            src_ref=half_sum.at[k, pl.ds(j * PIECE, PIECE)], dst_ref=xy_in.at[k, me_xy],
            send_sem=xy_send.at[k], recv_sem=xy_recv.at[k], device_id=dev, device_id_type=MESH,
        )

    def xy_all(k):
        return bulk(xy_in.at[k, 0 : NXY - 1], xy_send.at[k], xy_recv.at[k])

    def core_finish(k):
        c_copy(k).wait_recv()
        half_sum[k] = part[k, pl.ds(core * HALF, HALF)] + core_in[k]
        for j, dev in xy_peers:
            xy_copy(k, j, dev).start()

    def z_copy(k, j, dev):
        return pltpu.make_async_remote_copy(
            src_ref=z_in.at[k, me_z], dst_ref=z_in.at[k, me_z],
            send_sem=z_send.at[k], recv_sem=z_recv.at[k], device_id=dev, device_id_type=MESH,
        )

    def z_all(k):
        return bulk(z_in.at[k, 0 : NZZ - 1], z_send.at[k], z_recv.at[k])

    def xy_finish(k):
        xy_all(k).wait_recv()
        xy_in[k, me_xy] = half_sum[k, pl.ds(me_xy * PIECE, PIECE)]
        s = xy_in[k, 0]
        for j in range(1, NXY):
            s = s + xy_in[k, j]
        z_in[k, me_z] = s
        for j, dev in z_peers:
            z_copy(k, j, dev).start()

    def ga_at(j):
        return pl.ds(core * HALF + j * PIECE, PIECE)

    def ga_copy(k, j, dev):
        return pltpu.make_async_remote_copy(
            src_ref=total.at[k, ga_at(me_xy)], dst_ref=total.at[k, ga_at(me_xy)],
            send_sem=ga_send.at[k], recv_sem=ga_recv.at[k], device_id=dev, device_id_type=MESH,
        )

    def z_finish(k):
        z_all(k).wait_recv()
        s = z_in[k, 0]
        for j in range(1, NZZ):
            s = s + z_in[k, j]
        total[k, ga_at(me_xy)] = s
        for j, dev in xy_peers:
            ga_copy(k, j, dev).start()

    def gather_finish(k):
        bulk(total.at[k, 0 : HALF - PIECE], ga_send.at[k], ga_recv.at[k]).wait_recv()
        cg_half(k, core).start()

    def cg_half(k, which):
        return bulk(total.at[k, pl.ds(which * HALF, HALF)], cg_send.at[k], cg_recv.at[k])

    def ga_sent(k):
        bulk(total.at[k, 0 : HALF - PIECE], ga_send.at[k], ga_recv.at[k]).wait_send()

    def drain(k):
        st_all(k).wait_send()
        xy_all(k).wait_send()
        z_all(k).wait_send()
        c_copy(k).wait_send()

    def all_finish(k):
        cg_half(k, 1 - core).wait_recv()

    sides(him, 0, 0)
    lhs = jnp.concatenate(
        [
            jnp.concatenate(
                [
                    gim[zi + 1 - dz, C : 2 * C, NY * (2 - dx) : NY * (2 - dx) + L]
                    for dz in range(3)
                    for dx in range(3)
                ],
                axis=0,
            )
            for zi in range(1, NZ + 1)
        ],
        axis=1,
    )
    acc[...] = dot_nt(lhs, jnp.concatenate([him[zi] for zi in range(NZ)], axis=1))
    pack(0, 0, acc[0:SPLIT], slopes)
    pack(0, 1, acc[SPLIT : 2 * SPLIT], jnp.zeros((8, NY), F32))
    core_start(0)
    core_finish(0)

    slope, slope_dot = st_finish(1)
    spread(4, gain * inv_std)
    spread(5, slope)
    spread(6, slope_dot)

    def before(zi, carry):
        for xb in range(NX):
            at = slice(NY * xb, NY * (xb + 1))
            gp = cols[4] * (gh[zi, :, at] - cols[5] - pre[zi, :, at] * cols[6])
            pim[zi, C : 2 * C, NY * (xb + 1) : NY * (xb + 2)] = gp.astype(BF16)
        return carry

    lax.fori_loop(1, NZ + 1, before, 0)
    halo_start(*p_halo)

    def grad_one(p):
        def block(zi, i):
            b = 4 * p + i
            dz, dx = b // 3, b % 3
            return pim[zi + 1 - dz, C : 2 * C, pl.ds(pl.multiple_of(NY * (2 - dx), NY), L)]

        lhs = jnp.concatenate(
            [
                jnp.concatenate([block(zi, i) for i in range(5)], axis=0)
                for zi in range(1, NZ + 1)
            ],
            axis=1,
        )
        inner = slice(NY, NY + L)
        rhs = jnp.concatenate([xim[zi, :, inner] for zi in range(1, NZ + 1)], axis=1)
        acc[0 : 5 * C] = dot_nt(lhs, rhs)
        face = jnp.concatenate(
            [pim[1 + (NZ - 1) * p, C : 2 * C, NY * (2 - dx) : NY * (2 - dx) + L] for dx in range(3)], axis=0
        )
        rows = pl.ds(pl.multiple_of(2 * C * p, 8), 3 * C)
        acc[rows] += dot_nt(face, xim[(NZ + 1) * p, :, inner])
        pack(1, p, acc[pl.ds(pl.multiple_of((C // 2) * p, 8), SPLIT)], jnp.zeros((8, NY), F32))

    def two_halves(h, carry):
        grad_one(h * core + (1 - h) * (1 - core))

        @pl.when(h == 0)
        def _():
            core_start(1)
        return carry

    lax.fori_loop(0, 2, two_halves, 0)
    core_finish(1)

    xy_finish(0)
    sides(pim, 1, NY)
    conv_inner(pim, w1f, gh)
    xy_finish(1)
    z_finish(0)
    halo_wait(*p_halo)

    face_planes(hp, pim)
    conv_faces(pim, w1f, gh)

    def finish(zi, carry):
        for xb in range(NX):
            v = gh[zi, :, NY * xb : NY * (xb + 1)]
            up = gim[zi, C : 2 * C, NY * (xb + 1) : NY * (xb + 2)]
            tmp[pl.ds(xb, C, stride=NX), :] = v + up.astype(F32)
        out_ref[:, pl.ds(zi - 1, 1)] = tmp[...].reshape(C, 1, NX, NY).astype(BF16)
        return carry

    lax.fori_loop(1, NZ + 1, finish, 0)
    z_finish(1)
    gather_finish(0)
    all_finish(0)
    separate(total, 0, g2_ref)
    drain(0)
    drain(1)
    ga_sent(0)
    cg_half(0, core).wait_send()
    gather_finish(1)
    ga_sent(1)
    all_finish(1)
    cg_half(1, core).wait_send()


def separate(total, k, dst, done=None):
    main, tail = [], []
    for p in range(2):
        base = p * HALF
        rest = [total[k, base + SPLIT : base + SPLIT + 32, 16 * r : 16 * (r + 1)] for r in range(7)]
        rest[6] = rest[6][0 : SPLIT - 192]
        main.append(total[k, base : base + SPLIT])
        tail.append(jnp.concatenate(rest, axis=0))
    main, tail = jnp.concatenate(main, axis=0), jnp.concatenate(tail, axis=0)
    for b in range(9):
        rows = slice(b * C, (b + 1) * C)
        m = main[rows]
        dst[3 * b] = m[:, 0:C]
        dst[3 * b + 1] = m[:, C : 2 * C]
        dst[3 * b + 2] = jnp.concatenate([m[:, 2 * C : NY], tail[rows]], axis=1)
        if done is not None and b % 3 == 2:
            done(b // 3)


def results(
    raw, total, g2_raw, out_ref, g1_ref, g2_ref, gain_ref, bias_ref, g1, gain, bias, sem
):
    def copy(i, src, dst):
        each = pltpu.make_async_copy(src, dst, sem.at[i])
        each.start()
        return each

    copies = [copy(0, raw, out_ref), copy(1, g2_raw, g2_ref)]
    row = SPLIT + 32
    bias[...] = total[0, row : row + 1, 0:C]
    gain[...] = total[0, row + 1 : row + 2, 0:C]
    copies += [copy(2, gain, gain_ref), copy(3, bias, bias_ref)]

    def send(third):
        at = pl.ds(9 * third, 9)
        copies.append(copy(4 + third, g1.at[at], g1_ref.at[at]))

    separate(total, 1, g1, send)
    for each in copies:
        each.wait()


def local(features, upstream, weight_one, weight_two, norm_gain, norm_bias):
    w1 = jnp.transpose(weight_one, (2, 3, 4, 0, 1)).reshape(27, C, C)
    w2 = jnp.transpose(weight_two, (2, 3, 4, 0, 1)).reshape(27, C, C)
    vmem = pl.BlockSpec(memory_space=pltpu.VMEM)
    dma = pltpu.SemaphoreType.DMA
    far = pl.BlockSpec(memory_space=pltpu.HBM)
    raw, total, g2_raw = pl.pallas_call(
        kernel,
        out_shape=(
            pltpu.VMEM((C, NZ, NX, NY), BF16),
            pltpu.VMEM((2, ROWS, NY), F32),
            pltpu.VMEM((27, C, C), F32),
        ),
        in_specs=[far] * 6,
        out_specs=(vmem,) * 3,
        scratch_shapes=[
            pltpu.VMEM((C, NZ, NX, NY), BF16),
            pltpu.VMEM((C, NZ, NX, NY), BF16),
            pltpu.VMEM((27, C, C), BF16),
            pltpu.VMEM((27, C, C), BF16),
            pltpu.VMEM((1, C), F32),
            pltpu.VMEM((1, C), F32),
            dma((6,)),
            pltpu.VMEM((NZ + 2, 3 * C, LP), BF16),
            pltpu.VMEM((NZ + 2, 3 * C, LP), BF16),
            pltpu.VMEM((NZ, 3 * C, L), BF16),
            pltpu.VMEM((NZ + 2, 3 * C, LP), BF16),
            pltpu.VMEM((NZ + 2, C, L), F32),
            pltpu.VMEM((NZ + 2, C, L), F32),
            pltpu.VMEM((C * NX, NY), F32),
            pltpu.VMEM((2, C, L), BF16),
            pltpu.VMEM((2, C, L), BF16),
            pltpu.VMEM((2, C, L), BF16),
            pltpu.VMEM((3 * C, 9 * C), BF16),
            pltpu.VMEM((3 * C, 9 * C), BF16),
            pltpu.VMEM((3 * C, 9 * C), BF16),
            pltpu.VMEM((2, NSP, 8, NY), F32),
            pltpu.VMEM((7, C, NY), F32),
            pltpu.VMEM((9 * C, 3 * C), F32),
            pltpu.VMEM((2, ROWS, NY), F32),
            pltpu.VMEM((2, HALF, NY), F32),
            pltpu.VMEM((2, HALF, NY), F32),
            pltpu.VMEM((2, NXY, PIECE, NY), F32),
            pltpu.VMEM((2, NZZ, PIECE, NY), F32),
            dma((3, 2)), dma((3, 2)),
            dma((2,)), dma((2,)),
            dma((2,)), dma((2,)),
            dma((2,)), dma((2,)),
            dma((2,)), dma((2,)),
            dma((2,)), dma((2,)),
            dma((2,)), dma((2,)),
        ],
        compiler_params=pltpu.CompilerParams(
            collective_id=0, has_side_effects=True, vmem_limit_bytes=56 * 1024 * 1024
        ),
    )(
        features.reshape(C, NZ, NX, NY),
        upstream.reshape(C, NZ, NX, NY),
        w1,
        w2,
        norm_gain.reshape(1, C),
        norm_bias.reshape(1, C),
    )

    out, g1, g2, gain, bias = pl.pallas_call(
        results,
        out_shape=(
            jax.ShapeDtypeStruct((C, NZ, NX, NY), BF16),
            jax.ShapeDtypeStruct((27, C, C), F32),
            jax.ShapeDtypeStruct((27, C, C), F32),
            jax.ShapeDtypeStruct((1, C), F32),
            jax.ShapeDtypeStruct((1, C), F32),
        ),
        in_specs=[vmem] * 3,
        out_specs=(far,) * 5,
        scratch_shapes=[
            pltpu.VMEM((27, C, C), F32),
            pltpu.VMEM((1, C), F32),
            pltpu.VMEM((1, C), F32),
            dma((7,)),
        ],
    )(*(pltpu.with_memory_space_constraint(v, pltpu.VMEM) for v in (raw, total, g2_raw)))

    def grad(m):
        return jnp.transpose(m.reshape(3, 3, 3, C, C), (3, 4, 0, 1, 2))

    return out.reshape(1, C, NZ, NX, NY), grad(g1), grad(g2), gain.reshape(C), bias.reshape(C)


def solution(mesh):
    cells = P("dp", None, "space", None, None)
    return jax.shard_map(
        local,
        mesh=mesh,
        in_specs=(cells, cells, P(), P(), P(), P()),
        out_specs=(cells, P(), P(), P(), P()),
        check_vma=False,
    )
```
